512 devices in a mesh: grp: 16 (over y, core), exp: 32 (over x, z).
Axes of the slice: x: 4, y: 8, z: 8, core: 2. Of those that a mesh axis runs over, the one named last changes fastest.
Arguments:
- tokens: bfloat16 [67584, 4096], P(('grp', 'exp')), may hold values from -6 to 6
- routes: int32 [67584, 2], P(('grp', 'exp')), may hold values from 0 to 63, as said below
- gate_values: float32 [67584, 2], P(('grp', 'exp')), may hold values from 0.1 to 1
- dense_up: bfloat16 [4, 4096, 2688], P(None, ('grp', 'exp')), may hold values from -0.09375 to 0.09375
- dense_down: bfloat16 [4, 4096, 2688], P(None, ('grp', 'exp')), may hold values from -0.125 to 0.125
- up_noise: bfloat16 [4096, 10752], P(None, 'exp'), may hold values from -0.046875 to 0.046875
Outputs:
- mixed: bfloat16 [67584, 4096], P(('grp', 'exp'))
The draws below stay inside these ranges and needn't reach their ends.
Inputs may be any that keep to these rules, and one draw needn't show every extreme that they name: `routes`: each row names two different experts. The rows of one device name no expert more than 11 times, and in every group some expert below 4 is named exactly 11 times by each of the group's devices.
All inputs are finite; a program needn't handle non-finite values.
Results may differ from the reference program's by a relative error of at most 0.0067.
Values may be sent and summed in bfloat16 or wider, within the bound.
No kernel may reach another device: no remote copies, remote signals or barrier semaphores. Data moves between devices by JAX's collectives and lax.ppermute only.
A program may use at most 128 MiB of HBM per device.

```python
import math
import jax
import jax.numpy as jnp
from jax import lax

D = 4096
EXPERTS = 64
SHARDS = 8
HID_DEV = 336
HID = 2688
TOK_DEV = 132
CAP = 11
EXP_FLIGHT = 4
TOKENS = 67584
N_GRP = 16
N_EXP = 32


def draw_routes(key, part):
    key = jax.random.fold_in(key, 7)
    hot_key, perm_key, row_key, swap_key = jax.random.split(key, 4)
    device_count = N_GRP * N_EXP
    others = EXPERTS - 1
    hot_expert = jax.random.randint(hot_key, (N_GRP,), 0, EXP_FLIGHT)
    hot_device = jnp.repeat(hot_expert, N_EXP)
    orders = jax.vmap(lambda sub_key: jax.random.permutation(sub_key, others))(jax.random.split(perm_key, device_count))
    row_ids = jnp.arange(TOK_DEV)

    def choose(index):
        candidate = orders[:, jnp.mod(index, others)]
        return candidate + (candidate >= hot_device[:, None]).astype(jnp.int32)
    first_pick = jnp.where(row_ids[None, :] < CAP, hot_device[:, None], choose(row_ids - CAP))
    second = choose(TOK_DEV - CAP + row_ids)
    paired = jnp.stack([first_pick, second], axis=-1)
    row_order = jax.vmap(lambda sub_key: jax.random.permutation(sub_key, TOK_DEV))(jax.random.split(row_key, device_count))
    paired = jnp.take_along_axis(paired, row_order[:, :, None], axis=1)
    swap_bits = jax.random.randint(swap_key, (device_count, TOK_DEV, 1), 0, 2)
    paired = jnp.where(swap_bits == 1, paired[:, :, ::-1], paired)
    return paired.reshape(TOKENS, 2).astype(jnp.int32)


def steps_of(key, extent, shards, least, largest):
    gain = 1.0
    for axis_at, blocks in shards:
        draws = jax.random.uniform(jax.random.fold_in(jax.random.fold_in(key, 6), axis_at), (blocks,), jnp.float32, least / len(shards), largest / len(shards))
        gain = gain * jnp.repeat(jnp.exp(draws), extent[axis_at] // blocks).reshape((-1,) + (1,) * (len(extent) - 1 - axis_at))
    return gain


def bell_draw(key, shape, scale, limit, cuts=(), kind=jnp.bfloat16):
    loudness = steps_of(key, shape, cuts, -0.22, 0.18) if cuts else 1.0
    values = jax.random.normal(key, shape, jnp.float32) * scale * loudness
    return jnp.minimum(jnp.maximum(values, -limit), limit).astype(kind)


def setup_inputs(seed: int = 0) -> dict:
    streams_of = jax.random.split(jax.random.key(seed), 7)
    tokens = bell_draw(streams_of[0], (TOKENS, D), 1.0, 6.0, ((0, 512),))
    routes = draw_routes(jax.random.fold_in(streams_of[6], 71), 0)
    gate_values = jnp.clip(jnp.exp(math.log(1.0) - 2.3025851 * jax.random.uniform(streams_of[2], (TOKENS, 2), jnp.float32) ** steps_of(streams_of[2], (TOKENS, 2), ((0, 512),), -0.2, 0.2)), 0.1, 1.0)
    dense_up = bell_draw(streams_of[3], (EXP_FLIGHT, D, HID), D ** -0.5, 0.09375, ((1, 512),))
    dense_down = bell_draw(streams_of[4], (EXP_FLIGHT, D, HID), HID ** -0.5, 0.125, ((1, 512),))
    up_noise = bell_draw(streams_of[5], (D, EXP_FLIGHT * HID), (4 * D) ** -0.5, 0.046875, ((1, 32),))
    return dict(tokens=tokens, routes=routes, gate_values=gate_values, dense_up=dense_up, dense_down=dense_down, up_noise=up_noise)


def reference(tokens, routes, gate_values, dense_up, dense_down, up_noise):
    capacity_rows = N_GRP * N_EXP * CAP
    output = jnp.zeros((TOKENS, D), jnp.float32)
    for expert in range(EXP_FLIGHT):
        routed = jnp.any(routes == expert, axis=1)
        routed_int = routed.astype(jnp.int32)
        position = (jnp.cumsum(routed_int) - routed_int).astype(jnp.int32)
        target = jnp.where(routed, position, capacity_rows).astype(jnp.int32)
        gathered = jnp.zeros((capacity_rows + 1, D), jnp.bfloat16).at[target].set(tokens)[:capacity_rows]
        noise_cols = up_noise[:, expert * HID:(expert + 1) * HID]
        up_expert = (dense_up[expert].astype(jnp.float32) + noise_cols.astype(jnp.float32)).astype(jnp.bfloat16)
        preact = jnp.dot(gathered, up_expert, preferred_element_type=jnp.float32)
        hidden = jnp.square(jnp.maximum(preact, 0.0)).astype(jnp.bfloat16)
        down_expert = dense_down[expert]
        result = jnp.zeros((capacity_rows, D), jnp.float32)
        for block in range(SHARDS):
            lower = block * HID_DEV
            part = jnp.dot(hidden[:, lower:lower + HID_DEV], down_expert[:, lower:lower + HID_DEV].T,
                           preferred_element_type=jnp.float32)
            result = result + lax.optimization_barrier(part.astype(jnp.bfloat16)).astype(jnp.float32)
        weight = jnp.sum(jnp.where(routes == expert, gate_values, jnp.float32(0.0)), axis=1)
        picked = jnp.take(result, jnp.minimum(position, capacity_rows - 1).astype(jnp.int32), axis=0)
        output = output + weight[:, None] * picked
    return output.astype(jnp.bfloat16)
```

```python
import jax
import jax.numpy as jnp
from jax import lax
from jax.sharding import Mesh, PartitionSpec as P

SLOTS = 11


def on_device(tokens, routes, gate_values, dense_up, dense_down, up_noise):
    flight, rows, _ = dense_up.shape
    units = up_noise.shape[1]
    width = tokens.shape[1]
    toks = tokens.shape[0]
    blocks = dense_up.shape[2] // units

    def spread(w):
        return w.reshape(flight, rows, blocks, units).transpose(0, 2, 1, 3).reshape(flight * blocks, rows, units)

    pieces = jnp.concatenate([spread(dense_up), spread(dense_down)], axis=1)
    got = lax.all_to_all(pieces, ("x", "z"), 0, 0, tiled=True)
    owners = got.shape[0]
    span = owners * rows
    mine = lax.axis_index("y") * lax.axis_size("core") + lax.axis_index("core")
    noise = lax.dynamic_slice_in_dim(up_noise, mine * span, span, axis=0)
    up = got[:, :rows].reshape(span, units).astype(jnp.float32) + noise.astype(jnp.float32)
    up = up.astype(jnp.bfloat16)
    down = got[:, rows:].reshape(span, units)
    shard = jnp.stack([up.T, down.T])
    weights = lax.all_gather(shard, ("y", "core"))

    labels = jnp.arange(flight, dtype=jnp.int32)
    chosen = routes[:, :, None] == labels[None, None, :]
    present = jnp.any(chosen, axis=1).astype(jnp.int32)
    before = jnp.cumsum(present, axis=0) - present
    slot_ids = jnp.arange(SLOTS, dtype=jnp.int32)
    placed = present[:, :, None] * (before[:, :, None] == slot_ids[None, None, :]).astype(jnp.int32)
    selector = placed.reshape(toks, flight * SLOTS).astype(jnp.bfloat16)
    outgoing = lax.dot_general(
        selector, tokens, (((0,), (0,)), ((), ())), preferred_element_type=jnp.float32
    ).astype(jnp.bfloat16)
    routed = lax.all_to_all(outgoing.reshape(flight, SLOTS, width), "x", 0, 0, tiled=True)
    routed = routed.reshape(flight * SLOTS, width)
    everyone = lax.all_gather(routed, "z", axis=0, tiled=True)

    preact = jnp.einsum(
        "rgc,guc->ru", everyone.reshape(-1, weights.shape[0], span), weights[:, 0], preferred_element_type=jnp.float32
    )
    hidden = jnp.square(jnp.maximum(preact, 0.0)).astype(jnp.bfloat16)
    part = jnp.einsum("ru,guc->rgc", hidden, weights[:, 1], preferred_element_type=jnp.float32)
    part = part.astype(jnp.bfloat16).reshape(-1, flight * SLOTS, width)
    total = lax.psum_scatter(part, "z", scatter_dimension=0, tiled=False)
    home = lax.all_to_all(total.reshape(flight, SLOTS, width), "x", 0, 0, tiled=True)
    home = home.reshape(flight * SLOTS, width)
    gates = jnp.sum(jnp.where(chosen, gate_values[:, :, None], jnp.float32(0.0)), axis=1)
    mixing = (placed.astype(jnp.float32) * gates[:, :, None]).reshape(toks, flight * SLOTS)
    mixed = jnp.dot(mixing, home.astype(jnp.float32), precision=lax.Precision.HIGHEST, preferred_element_type=jnp.float32)
    return mixed.astype(jnp.bfloat16)


def solution(mesh):
    split = Mesh(mesh.devices.reshape(8, 2, 4, 8), ("y", "core", "x", "z"))
    every = ("y", "core", "x", "z")
    return jax.shard_map(
        on_device,
        mesh=split,
        in_specs=(
            P(every, None),
            P(every, None),
            P(every, None),
            P(None, every, None),
            P(None, every, None),
            P(None, ("x", "z")),
        ),
        out_specs=P(every, None),
        check_vma=False,
    )
```

```python
import jax, jax.numpy as jnp
from jax import lax
from jax.experimental import pallas as pl
from jax.experimental.pallas import tpu as pltpu
from jax.sharding import Mesh, PartitionSpec as P

F32, BF16 = jnp.float32, jnp.bfloat16
SLOTS, PITCH, FLIGHT = 11, 12, 4
VMEM_LIMIT = 48 * 1024 * 1024


def place(routes):
    toks = routes.shape[1]
    rows = FLIGHT * PITCH
    slot = lax.broadcasted_iota(jnp.int32, (rows, toks), 0)
    expert = sum((slot >= PITCH * e).astype(jnp.int32) for e in range(1, FLIGHT))
    slot = slot - PITCH * expert
    first, second = routes[0:1] == expert, routes[1:2] == expert
    present = jnp.logical_or(first, second)
    earlier = lax.broadcasted_iota(jnp.int32, (toks, toks), 0) < lax.broadcasted_iota(jnp.int32, (toks, toks), 1)
    before = jnp.dot(
        present.astype(F32).astype(BF16), earlier.astype(F32).astype(BF16), preferred_element_type=F32
    )
    taken = jnp.logical_and(present, before == slot.astype(F32))
    return taken, first, second


def dispatch_kernel(routes_ref, tokens_ref, out_ref, shrink_ref, *, dtype):
    taken, _, _ = place(routes_ref[...])
    picked = jnp.dot(taken.astype(F32).astype(BF16), tokens_ref[...], preferred_element_type=F32)
    top = jnp.max(jnp.abs(picked), axis=1, keepdims=True)
    grow, shrink = jnp.ones_like(top), jnp.ones_like(top)
    for bits in (32, 16, 8, 4, 2, 1):
        low = top * (2.0**bits) < 16384.0
        factor = jnp.where(low, 2.0**bits, 1.0)
        top, grow = top * factor, grow * factor
        shrink = shrink * jnp.where(low, 2.0**-bits, 1.0)
    shrink_ref[...] = shrink
    picked = (picked * grow).astype(dtype)
    for e in range(FLIGHT):
        out_ref[e] = picked[e * PITCH : (e + 1) * PITCH]


def dispatch(routes_t, tokens, dtype):
    toks, width = tokens.shape
    return pl.pallas_call(
        lambda *r: dispatch_kernel(*r, dtype=dtype),
        out_shape=(
            jax.ShapeDtypeStruct((FLIGHT, PITCH, width), dtype),
            jax.ShapeDtypeStruct((FLIGHT * PITCH, 1), F32),
        ),
        compiler_params=pltpu.CompilerParams(vmem_limit_bytes=VMEM_LIMIT),
    )(routes_t, tokens)


def prepare_kernel(mine_ref, got_ref, noise_ref, out_ref):
    units, span = out_ref.shape[1:]
    rows = span // got_ref.shape[0]
    got = got_ref[...].reshape(2 * span, units)
    src = lax.broadcasted_iota(jnp.int32, (2 * span, span), 0)
    dst = lax.broadcasted_iota(jnp.int32, (2 * span, span), 1)
    dst = dst + (dst & ~(rows - 1))
    ups = (src == dst).astype(F32).astype(BF16)
    downs = (src == dst + rows).astype(F32).astype(BF16)
    up = lax.dot_general(ups, got, (((0,), (0,)), ((), ())), preferred_element_type=F32)
    up = (up + noise_ref[...].astype(F32)).astype(BF16)
    same = lax.broadcasted_iota(jnp.int32, (span, span), 0) == lax.broadcasted_iota(jnp.int32, (span, span), 1)
    same = same.astype(F32).astype(BF16)
    turn = (((0,), (0,)), ((), ()))
    out_ref[0] = lax.dot_general(up, same, turn, preferred_element_type=F32).astype(BF16)
    out_ref[1] = lax.dot_general(got, downs, turn, preferred_element_type=F32).astype(BF16)


def prepare(mine, got, noise):
    owners, both, units = got.shape
    span = owners * both // 2
    return pl.pallas_call(
        prepare_kernel,
        grid_spec=pltpu.PrefetchScalarGridSpec(
            num_scalar_prefetch=1,
            grid=(1,),
            in_specs=[
                pl.BlockSpec((owners, both, units), lambda i, m: (0, 0, 0)),
                pl.BlockSpec((span, units), lambda i, m: (m[0], 0)),
            ],
            out_specs=pl.BlockSpec((2, units, span), lambda i, m: (0, 0, 0)),
        ),
        out_shape=jax.ShapeDtypeStruct((2, units, span), BF16),
        compiler_params=pltpu.CompilerParams(vmem_limit_bytes=VMEM_LIMIT),
    )(mine, got, noise)


def expert_kernel(half, x_ref, w_ref, out_ref, acc_ref, hid_ref):
    step = pl.program_id(0)
    group, _, units, span = w_ref.shape

    @pl.when(step < half)
    def _():
        total = None
        for g in range(group):
            x = x_ref[:, g * span : (g + 1) * span].astype(F32).astype(BF16)
            term = lax.dot_general(x, w_ref[g, 0], (((1,), (1,)), ((), ())), preferred_element_type=F32)
            total = term if total is None else total + term

        @pl.when(step == 0)
        def _():
            acc_ref[...] = total

        @pl.when(step > 0)
        def _():
            acc_ref[...] += total

        @pl.when(step == half - 1)
        def _():
            hid_ref[...] = jnp.square(jnp.maximum(acc_ref[...], 0.0)).astype(BF16)

    @pl.when(step >= half)
    def _():
        for g in range(group):
            out_ref[:, g * span : (g + 1) * span] = jnp.dot(
                hid_ref[...], w_ref[g, 0], preferred_element_type=F32
            ).astype(BF16)


def expert(x, w, group=4):
    rows, width = x.shape
    members, _, units, span = w.shape
    half = members // group
    cols = group * span
    return pl.pallas_call(
        lambda *r: expert_kernel(half, *r),
        grid=(2 * half,),
        in_specs=[
            pl.BlockSpec((rows, cols), lambda i: (0, jnp.minimum(i, half - 1))),
            pl.BlockSpec((group, 1, units, span), lambda i: (i % half, i // half, 0, 0)),
        ],
        out_specs=pl.BlockSpec((rows, cols), lambda i: (0, jnp.maximum(i - half, 0))),
        out_shape=jax.ShapeDtypeStruct((rows, width), BF16),
        scratch_shapes=[pltpu.VMEM((rows, units), F32), pltpu.VMEM((rows, units), BF16)],
        compiler_params=pltpu.CompilerParams(vmem_limit_bytes=VMEM_LIMIT),
        cost_estimate=pl.CostEstimate(flops=4 * rows * width * units, bytes_accessed=4 * rows * width + 4 * width * units, transcendentals=0),
    )(x, w)


def mix_kernel(routes_ref, gates_ref, shrink_ref, home_ref, out_ref):
    taken, first, second = place(routes_ref[...])
    gates = gates_ref[...]
    weight = jnp.where(first, gates[0:1], 0.0) + jnp.where(second, gates[1:2], 0.0)
    weight = jnp.where(taken, weight, 0.0) * shrink_ref[...]
    high = weight.astype(BF16)
    rest = weight - high.astype(F32)
    middle = rest.astype(BF16)
    low = (rest - middle.astype(F32)).astype(BF16)
    home = jnp.concatenate([home_ref[e].astype(F32) for e in range(FLIGHT)], axis=0)
    home = (home * shrink_ref[...]).astype(BF16)
    turn = (((0,), (0,)), ((), ()))
    total = None
    for part in (low, middle, high):
        term = lax.dot_general(part, home, turn, preferred_element_type=F32)
        total = term if total is None else total + term
    out_ref[...] = total.astype(BF16)


def mix(routes_t, gates_t, shrink, home):
    toks, width = routes_t.shape[1], home.shape[2]
    return pl.pallas_call(
        mix_kernel,
        out_shape=jax.ShapeDtypeStruct((toks, width), BF16),
        compiler_params=pltpu.CompilerParams(vmem_limit_bytes=VMEM_LIMIT),
    )(routes_t, gates_t, shrink, home)


def on_device(tokens, routes, gate_values, dense_up, dense_down, up_noise):
    flight, rows, _ = dense_up.shape
    units = up_noise.shape[1]
    width = tokens.shape[1]
    blocks = dense_up.shape[2] // units

    def spread(w):
        return w.reshape(flight, rows, blocks, units).transpose(0, 2, 1, 3).reshape(flight * blocks, rows, units)

    pieces = jnp.concatenate([spread(dense_up), spread(dense_down)], axis=1)
    got = lax.all_to_all(pieces, ("x", "z"), 0, 0, tiled=True)
    mine = lax.axis_index("y") * lax.axis_size("core") + lax.axis_index("core")
    shard = prepare(mine.reshape(1), got, up_noise)

    outgoing, shrink = dispatch(routes.T, tokens, BF16)
    shard, outgoing = lax.optimization_barrier((shard, outgoing))
    weights = lax.all_gather(shard, ("y", "core"))
    routed = lax.all_to_all(outgoing, "x", 0, 0, tiled=True)
    routed = routed.reshape(flight * PITCH, width).astype(jnp.float16)
    everyone = lax.all_gather(routed, "z", axis=0, tiled=True).astype(BF16)

    part = expert(everyone, weights, 8)
    total = lax.psum_scatter(part, "z", scatter_dimension=0, tiled=True)
    home = lax.all_to_all(total.reshape(flight, PITCH, width), "x", 0, 0, tiled=True)
    return mix(routes.T, gate_values.T, shrink, home)


def solution(mesh):
    split = Mesh(mesh.devices.reshape(8, 2, 4, 8), ("y", "core", "x", "z"))
    every = ("y", "core", "x", "z")
    return jax.shard_map(
        on_device,
        mesh=split,
        in_specs=(
            P(every, None),
            P(every, None),
            P(every, None),
            P(None, every, None),
            P(None, every, None),
            P(None, ("x", "z")),
        ),
        out_specs=P(every, None),
        check_vma=False,
    )
```

```python
import jax, jax.numpy as jnp
from jax import lax
from jax.experimental import pallas as pl
from jax.experimental.pallas import tpu as pltpu
from jax.sharding import Mesh, PartitionSpec as P

F32, BF16 = jnp.float32, jnp.bfloat16
SLOTS, PITCH, FLIGHT = 11, 12, 4
VMEM_LIMIT = 48 * 1024 * 1024


def place(routes):
    toks = routes.shape[1]
    rows = FLIGHT * PITCH
    slot = lax.broadcasted_iota(jnp.int32, (rows, toks), 0)
    expert = sum((slot >= PITCH * e).astype(jnp.int32) for e in range(1, FLIGHT))
    slot = slot - PITCH * expert
    first, second = routes[0:1] == expert, routes[1:2] == expert
    present = jnp.logical_or(first, second)
    earlier = lax.broadcasted_iota(jnp.int32, (toks, toks), 0) < lax.broadcasted_iota(jnp.int32, (toks, toks), 1)
    before = jnp.dot(
        present.astype(F32).astype(BF16), earlier.astype(F32).astype(BF16), preferred_element_type=F32
    )
    taken = jnp.logical_and(present, before == slot.astype(F32))
    return taken, first, second


def dispatch_kernel(routes_ref, tokens_ref, out_ref, shrink_ref, *, dtype):
    taken, _, _ = place(routes_ref[...])
    picked = jnp.dot(taken.astype(F32).astype(BF16), tokens_ref[...], preferred_element_type=F32)
    top = jnp.max(jnp.abs(picked), axis=1, keepdims=True)
    grow, shrink = jnp.ones_like(top), jnp.ones_like(top)
    for bits in (32, 16, 8, 4, 2, 1):
        low = top * (2.0**bits) < 16384.0
        factor = jnp.where(low, 2.0**bits, 1.0)
        top, grow = top * factor, grow * factor
        shrink = shrink * jnp.where(low, 2.0**-bits, 1.0)
    shrink_ref[...] = shrink
    picked = (picked * grow).astype(dtype)
    for e in range(FLIGHT):
        out_ref[e] = picked[e * PITCH : (e + 1) * PITCH]


def dispatch(routes_t, tokens, dtype):
    toks, width = tokens.shape
    return pl.pallas_call(
        lambda *r: dispatch_kernel(*r, dtype=dtype),
        out_shape=(
            jax.ShapeDtypeStruct((FLIGHT, PITCH, width), dtype),
            jax.ShapeDtypeStruct((FLIGHT * PITCH, 1), F32),
        ),
        compiler_params=pltpu.CompilerParams(vmem_limit_bytes=VMEM_LIMIT),
    )(routes_t, tokens)


def split_kernel(up_ref, down_ref, out_ref):
    flight = up_ref.shape[0]
    units = out_ref.shape[2]
    blocks = out_ref.shape[0] // flight
    for e in range(flight):
        both = jnp.concatenate([up_ref[e].astype(F32), down_ref[e].astype(F32)], axis=0).astype(BF16)
        for b in range(blocks):
            out_ref[e * blocks + b] = both[:, b * units : (b + 1) * units]


def split(up, down, units):
    flight, rows, total = up.shape
    return pl.pallas_call(
        split_kernel,
        out_shape=jax.ShapeDtypeStruct((flight * total // units, 2 * rows, units), BF16),
        compiler_params=pltpu.CompilerParams(vmem_limit_bytes=VMEM_LIMIT),
    )(up, down)


def prepare_kernel(mine_ref, got_ref, noise_ref, out_ref):
    units, span = out_ref.shape[1:]
    rows = span // got_ref.shape[0]
    got = got_ref[...].reshape(2 * span, units)
    src = lax.broadcasted_iota(jnp.int32, (2 * span, span), 0)
    dst = lax.broadcasted_iota(jnp.int32, (2 * span, span), 1)
    dst = dst + (dst & ~(rows - 1))
    ups = (src == dst).astype(F32).astype(BF16)
    downs = (src == dst + rows).astype(F32).astype(BF16)
    turn = (((0,), (0,)), ((), ()))
    up = lax.dot_general(got, ups, turn, preferred_element_type=F32)
    out_ref[0] = (up + noise_ref[...].astype(F32)).astype(BF16)
    out_ref[1] = lax.dot_general(got, downs, turn, preferred_element_type=F32).astype(BF16)


def prepare(mine, got, noise_t):
    owners, both, units = got.shape
    span = owners * both // 2
    return pl.pallas_call(
        prepare_kernel,
        grid_spec=pltpu.PrefetchScalarGridSpec(
            num_scalar_prefetch=1,
            grid=(1,),
            in_specs=[
                pl.BlockSpec((owners, both, units), lambda i, m: (0, 0, 0)),
                pl.BlockSpec((units, span), lambda i, m: (0, m[0])),
            ],
            out_specs=pl.BlockSpec((2, units, span), lambda i, m: (0, 0, 0)),
        ),
        out_shape=jax.ShapeDtypeStruct((2, units, span), BF16),
        compiler_params=pltpu.CompilerParams(vmem_limit_bytes=VMEM_LIMIT),
    )(mine, got, noise_t)


def expert_kernel(half, x_ref, w_ref, out_ref, acc_ref, hid_ref):
    step = pl.program_id(0)
    group, _, units, span = w_ref.shape

    @pl.when(step < half)
    def _():
        total = None
        for g in range(group):
            x = x_ref[:, g * span : (g + 1) * span].astype(F32).astype(BF16)
            term = lax.dot_general(x, w_ref[g, 0], (((1,), (1,)), ((), ())), preferred_element_type=F32)
            total = term if total is None else total + term

        @pl.when(step == 0)
        def _():
            acc_ref[...] = total

        @pl.when(step > 0)
        def _():
            acc_ref[...] += total

        @pl.when(step == half - 1)
        def _():
            hid_ref[...] = jnp.square(jnp.maximum(acc_ref[...], 0.0)).astype(BF16)

    @pl.when(step >= half)
    def _():
        for g in range(group):
            out_ref[:, g * span : (g + 1) * span] = jnp.dot(
                hid_ref[...], w_ref[g, 0], preferred_element_type=F32
            ).astype(BF16)


def expert(x, w, group=4):
    rows, width = x.shape
    members, _, units, span = w.shape
    half = members // group
    cols = group * span
    return pl.pallas_call(
        lambda *r: expert_kernel(half, *r),
        grid=(2 * half,),
        in_specs=[
            pl.BlockSpec((rows, cols), lambda i: (0, jnp.minimum(i, half - 1))),
            pl.BlockSpec((group, 1, units, span), lambda i: (i % half, i // half, 0, 0)),
        ],
        out_specs=pl.BlockSpec((rows, cols), lambda i: (0, jnp.maximum(i - half, 0))),
        out_shape=jax.ShapeDtypeStruct((rows, width), BF16),
        scratch_shapes=[pltpu.VMEM((rows, units), F32), pltpu.VMEM((rows, units), BF16)],
        compiler_params=pltpu.CompilerParams(vmem_limit_bytes=VMEM_LIMIT),
        cost_estimate=pl.CostEstimate(flops=4 * rows * width * units, bytes_accessed=4 * rows * width + 4 * width * units, transcendentals=0),
    )(x, w)


def mix_kernel(routes_ref, gates_ref, shrink_ref, home_ref, out_ref):
    taken, first, second = place(routes_ref[...])
    gates = gates_ref[...]
    weight = jnp.where(first, gates[0:1], 0.0) + jnp.where(second, gates[1:2], 0.0)
    weight = jnp.where(taken, weight, 0.0) * shrink_ref[...]
    high = weight.astype(BF16)
    rest = weight - high.astype(F32)
    middle = rest.astype(BF16)
    low = (rest - middle.astype(F32)).astype(BF16)
    home = jnp.concatenate([home_ref[e].astype(F32) for e in range(FLIGHT)], axis=0)
    home = (home * shrink_ref[...]).astype(BF16)
    turn = (((0,), (0,)), ((), ()))
    total = None
    for part in (low, middle, high):
        term = lax.dot_general(part, home, turn, preferred_element_type=F32)
        total = term if total is None else total + term
    out_ref[...] = total.astype(BF16)


def mix(routes_t, gates_t, shrink, home):
    toks, width = routes_t.shape[1], home.shape[2]
    return pl.pallas_call(
        mix_kernel,
        out_shape=jax.ShapeDtypeStruct((toks, width), BF16),
        compiler_params=pltpu.CompilerParams(vmem_limit_bytes=VMEM_LIMIT),
    )(routes_t, gates_t, shrink, home)


def on_device(tokens, routes, gate_values, dense_up, dense_down, up_noise):
    flight = dense_up.shape[0]
    units = up_noise.shape[1]
    width = tokens.shape[1]

    got = lax.all_to_all(split(dense_up, dense_down, units), ("x", "z"), 0, 0, tiled=True)
    mine = lax.axis_index("y") * lax.axis_size("core") + lax.axis_index("core")
    shard = prepare(mine.reshape(1), got, up_noise.T)

    outgoing, shrink = dispatch(routes.T, tokens, BF16)
    here = lax.axis_index("x")
    near = []
    for s in range(flight):
        block = lax.dynamic_index_in_dim(outgoing, (here + s) % flight, 0, keepdims=False)
        near.append(lax.ppermute(block, "x", [(i, (i + s) % flight) for i in range(flight)]) if s else block)
    shard, near = lax.optimization_barrier((shard, near))
    weights = lax.all_gather(shard, ("y", "core"))
    routed = [
        lax.select_n(here, *[near[(x - k) % flight] for x in range(flight)]) for k in range(flight)
    ]
    routed = jnp.concatenate(routed, axis=0).astype(jnp.float16)
    everyone = lax.all_gather(routed, "z", axis=0, tiled=True).astype(BF16)

    part = expert(everyone, weights, 8)
    total = lax.psum_scatter(part, "z", scatter_dimension=0, tiled=True)
    home = lax.all_to_all(total.reshape(flight, PITCH, width), "x", 0, 0, tiled=True)
    return mix(routes.T, gate_values.T, shrink, home)


def solution(mesh):
    split = Mesh(mesh.devices.reshape(8, 2, 4, 8), ("y", "core", "x", "z"))
    every = ("y", "core", "x", "z")
    return jax.shard_map(
        on_device,
        mesh=split,
        in_specs=(
            P(every, None),
            P(every, None),
            P(every, None),
            P(None, every, None),
            P(None, every, None),
            P(None, ("x", "z")),
        ),
        out_specs=P(every, None),
        check_vma=False,
    )
```

```python
import jax, jax.numpy as jnp
from jax import lax
from jax.experimental import pallas as pl
from jax.experimental.pallas import tpu as pltpu
from jax.sharding import Mesh, PartitionSpec as P

F32, BF16 = jnp.float32, jnp.bfloat16
PITCH, FLIGHT = 12, 4
HID_LANES, UP_ROWS = 384, 344
VMEM_LIMIT = 48 * 1024 * 1024


def place(routes):
    toks = routes.shape[1]
    rows = FLIGHT * PITCH
    slot = lax.broadcasted_iota(jnp.int32, (rows, toks), 0)
    expert = sum((slot >= PITCH * e).astype(jnp.int32) for e in range(1, FLIGHT))
    slot = slot - PITCH * expert
    first, second = routes[0:1] == expert, routes[1:2] == expert
    present = jnp.logical_or(first, second)
    earlier = lax.broadcasted_iota(jnp.int32, (toks, toks), 0) < lax.broadcasted_iota(jnp.int32, (toks, toks), 1)
    before = jnp.dot(
        present.astype(F32).astype(BF16), earlier.astype(F32).astype(BF16), preferred_element_type=F32
    )
    taken = jnp.logical_and(present, before == slot.astype(F32))
    return taken, first, second


def rescale(top):
    factor, power = jnp.ones_like(top), jnp.zeros_like(top)
    for bits in (32, 16, 8, 4, 2, 1):
        high = top * (2.0**-bits) >= 8192.0
        scale = jnp.where(high, 2.0**-bits, 1.0)
        top, factor = top * scale, factor * scale
        power = power - jnp.where(high, float(bits), 0.0)
    for bits in (32, 16, 8, 4, 2, 1):
        low = top * (2.0**bits) < 16384.0
        scale = jnp.where(low, 2.0**bits, 1.0)
        top, factor = top * scale, factor * scale
        power = power + jnp.where(low, float(bits), 0.0)
    return factor, power


def dispatch_kernel(routes_ref, tokens_ref, out_ref):
    taken, _, _ = place(routes_ref[...])
    picked = jnp.dot(taken.astype(F32).astype(BF16), tokens_ref[...], preferred_element_type=F32).astype(BF16)
    for e in range(FLIGHT):
        out_ref[e] = picked[e * PITCH : (e + 1) * PITCH]


def dispatch(routes_t, tokens):
    return pl.pallas_call(
        dispatch_kernel,
        out_shape=jax.ShapeDtypeStruct((FLIGHT, PITCH, tokens.shape[1]), BF16),
        compiler_params=pltpu.CompilerParams(vmem_limit_bytes=VMEM_LIMIT),
    )(routes_t, tokens)


def split_kernel(up_ref, out_ref):
    flight = up_ref.shape[0]
    units = out_ref.shape[2]
    blocks = out_ref.shape[0] // flight
    for e in range(flight):
        for b in range(blocks):
            out_ref[e * blocks + b] = up_ref[e, :, b * units : (b + 1) * units]


def split(up, units):
    flight, rows, total = up.shape
    return pl.pallas_call(
        split_kernel,
        out_shape=jax.ShapeDtypeStruct((flight * total // units, rows, units), BF16),
        compiler_params=pltpu.CompilerParams(vmem_limit_bytes=VMEM_LIMIT),
    )(up)


def prepare_kernel(mine_ref, got_ref, noise_ref, out_ref):
    owners, rows, units = got_ref.shape
    span = owners * rows
    got = got_ref[...].astype(F32).reshape(span, units).astype(BF16)
    same = lax.broadcasted_iota(jnp.int32, (span, span), 0) == lax.broadcasted_iota(jnp.int32, (span, span), 1)
    same = same.astype(F32).astype(BF16)
    up = lax.dot_general(got, same, (((0,), (0,)), ((), ())), preferred_element_type=F32)
    up = (up + noise_ref[...].astype(F32)).astype(BF16).astype(F32)
    top = jnp.max(jnp.max(jnp.abs(up), axis=1, keepdims=True), axis=0, keepdims=True)
    factor, power = rescale(top)
    power = jnp.broadcast_to(power, (out_ref.shape[0] - units, span))
    out_ref[...] = jnp.concatenate([up * factor, power], axis=0).astype(BF16)


def prepare(mine, got, noise_t):
    owners, rows, units = got.shape
    span = owners * rows
    return pl.pallas_call(
        prepare_kernel,
        grid_spec=pltpu.PrefetchScalarGridSpec(
            num_scalar_prefetch=1,
            grid=(1,),
            in_specs=[
                pl.BlockSpec((owners, rows, units), lambda i, m: (0, 0, 0)),
                pl.BlockSpec((units, span), lambda i, m: (0, m[0])),
            ],
            out_specs=pl.BlockSpec((UP_ROWS, span), lambda i, m: (0, 0)),
        ),
        out_shape=jax.ShapeDtypeStruct((UP_ROWS, span), BF16),
        compiler_params=pltpu.CompilerParams(vmem_limit_bytes=VMEM_LIMIT),
    )(mine, got, noise_t)


def up_kernel(x_ref, w_ref, out_ref, acc_ref):
    step = pl.program_id(0)
    group, units, span = w_ref.shape
    total = None
    for g in range(group):
        x = x_ref[:, g * span : (g + 1) * span]
        term = lax.dot_general(x, w_ref[g], (((1,), (1,)), ((), ())), preferred_element_type=F32)
        total = term if total is None else total + term

    @pl.when(step == 0)
    def _():
        acc_ref[...] = total

    @pl.when(step > 0)
    def _():
        acc_ref[...] += total

    @pl.when(step == pl.num_programs(0) - 1)
    def _():
        hidden = jnp.square(jnp.maximum(acc_ref[...], 0.0))
        factor, power = rescale(jnp.max(hidden, axis=1, keepdims=True))
        hidden = hidden.astype(BF16).astype(F32) * factor
        power = jnp.broadcast_to(power, (power.shape[0], out_ref.shape[1] - units))
        out_ref[...] = jnp.concatenate([hidden, power], axis=1).astype(BF16)


def up_project(x, w, group=8):
    rows, width = x.shape
    members, units, span = w.shape
    return pl.pallas_call(
        up_kernel,
        grid=(members // group,),
        in_specs=[
            pl.BlockSpec((rows, group * span), lambda i: (0, i)),
            pl.BlockSpec((group, units, span), lambda i: (i, 0, 0)),
        ],
        out_specs=pl.BlockSpec((rows, HID_LANES), lambda i: (0, 0)),
        out_shape=jax.ShapeDtypeStruct((rows, HID_LANES), BF16),
        scratch_shapes=[pltpu.VMEM((rows, units), F32)],
        compiler_params=pltpu.CompilerParams(vmem_limit_bytes=VMEM_LIMIT),
        cost_estimate=pl.CostEstimate(flops=2 * rows * width * units, bytes_accessed=2 * width * (rows + units), transcendentals=0),
    )(x, w)


def down_kernel(units, hid_ref, w_ref, out_ref):
    blocks = hid_ref.shape[0]
    hidden = []
    for b in range(blocks):
        h = hid_ref[b].astype(F32)
        hidden.append(h[:, :units] * jnp.exp2(-h[:, units : units + 1]))
    hidden = jnp.concatenate(hidden, axis=1).astype(BF16)
    w = w_ref[...].reshape(-1, w_ref.shape[2])
    out = lax.dot_general(hidden, w, (((1,), (1,)), ((), ())), preferred_element_type=F32).astype(BF16)
    for z in range(blocks):
        for x in range(FLIGHT):
            first = (z * FLIGHT + x) * PITCH
            out_ref[x * blocks + z] = out[first : first + PITCH]


def down_project(hid, w, units):
    blocks, rows, lanes = hid.shape
    members, count, total = w.shape
    cols = members * count
    return pl.pallas_call(
        lambda *r: down_kernel(units, *r),
        out_shape=jax.ShapeDtypeStruct((rows // PITCH, PITCH, cols), BF16),
        compiler_params=pltpu.CompilerParams(vmem_limit_bytes=VMEM_LIMIT),
        cost_estimate=pl.CostEstimate(flops=2 * rows * cols * total, bytes_accessed=2 * cols * total + 2 * blocks * rows * lanes, transcendentals=0),
    )(hid, w)


def mix_kernel(rows, routes_ref, gates_ref, home_ref, out_ref):
    taken, first, second = place(routes_ref[...])
    gates = gates_ref[...]
    weight = jnp.where(first, gates[0:1], 0.0) + jnp.where(second, gates[1:2], 0.0)
    weight = jnp.where(taken, weight, 0.0)
    high = weight.astype(BF16)
    rest = weight - high.astype(F32)
    middle = rest.astype(BF16)
    low = (rest - middle.astype(F32)).astype(BF16)
    owners, _, cols = home_ref.shape
    blocks = owners // FLIGHT
    home = []
    for b in range(blocks):
        home.append(jnp.concatenate([home_ref[e * blocks + b].astype(F32) for e in range(FLIGHT)], axis=0))
    piece = cols // blocks
    src = lax.broadcasted_iota(jnp.int32, (cols, cols), 0)
    dst = lax.broadcasted_iota(jnp.int32, (cols, cols), 1)
    block, rem = src // piece, src % piece
    order = (dst == rem // rows * (blocks * rows) + block * rows + rem % rows).astype(F32).astype(BF16)
    turn = (((0,), (0,)), ((), ()))
    for q in range(blocks):
        chunk = jnp.concatenate([h[:, q * piece : (q + 1) * piece] for h in home], axis=1).astype(BF16)
        chunk = jnp.dot(chunk, order, preferred_element_type=F32).astype(BF16)
        total = None
        for part in (low, middle, high):
            term = lax.dot_general(part, chunk, turn, preferred_element_type=F32)
            total = term if total is None else total + term
        out_ref[:, q * cols : (q + 1) * cols] = total.astype(BF16)


def mix(routes_t, gates_t, home, rows):
    toks = routes_t.shape[1]
    owners, _, cols = home.shape
    return pl.pallas_call(
        lambda *r: mix_kernel(rows, *r),
        out_shape=jax.ShapeDtypeStruct((toks, owners // FLIGHT * cols), BF16),
        compiler_params=pltpu.CompilerParams(vmem_limit_bytes=VMEM_LIMIT),
    )(routes_t, gates_t, home)


def on_device(tokens, routes, gate_values, dense_up, dense_down, up_noise):
    flight, rows, total = dense_up.shape
    units = up_noise.shape[1]
    blocks = total // units
    width = tokens.shape[1]
    here = lax.axis_index("x")
    mine = lax.axis_index("y") * lax.axis_size("core") + lax.axis_index("core")

    outgoing = dispatch(routes.T, tokens)
    routed = lax.all_to_all(outgoing, "x", 0, 0, tiled=True).reshape(flight * PITCH, width)
    everyone = lax.all_gather(routed, "z", axis=0, tiled=True)

    pieces, _ = lax.optimization_barrier((split(dense_up, units), routed))
    got = lax.all_to_all(pieces, ("x", "z"), 0, 0, tiled=True)
    near = []
    for s in range(flight):
        block = lax.dynamic_index_in_dim(dense_down, (here + s) % flight, 0, keepdims=False)
        near.append(lax.ppermute(block, "x", [(i, (i + s) % flight) for i in range(flight)]) if s else block)
    got, near = lax.optimization_barrier((got, near))
    shard = prepare(mine.reshape(1), got, up_noise.T).astype(jnp.float16)
    up = lax.all_gather(shard, ("y", "core"))
    power = up[:, units : units + 1, :1].astype(F32)
    up = (up[:, :units].astype(F32) * jnp.exp2(-power)).astype(BF16)
    down = [lax.select_n(here, *[near[(x - k) % flight] for x in range(flight)]) for k in range(flight)]
    down = lax.all_gather(jnp.concatenate(down, axis=0), ("y", "core"))

    hidden = up_project(everyone, up).astype(jnp.float16)
    hidden = lax.all_gather(hidden, "z", axis=0, tiled=True).astype(BF16)
    out = down_project(hidden.reshape(blocks, -1, HID_LANES), down, units)
    home = lax.all_to_all(out, ("x", "z"), 0, 0, tiled=True)
    return mix(routes.T, gate_values.T, home, rows)


def solution(mesh):
    split = Mesh(mesh.devices.reshape(8, 2, 4, 8), ("y", "core", "x", "z"))
    every = ("y", "core", "x", "z")
    return jax.shard_map(
        on_device,
        mesh=split,
        in_specs=(
            P(every, None),
            P(every, None),
            P(every, None),
            P(None, every, None),
            P(None, every, None),
            P(None, ("x", "z")),
        ),
        out_specs=P(every, None),
        check_vma=False,
    )
```

```python
import jax, jax.numpy as jnp
from jax import lax
from jax.experimental import pallas as pl
from jax.experimental.pallas import tpu as pltpu
from jax.sharding import Mesh, PartitionSpec as P

F32, BF16 = jnp.float32, jnp.bfloat16
PITCH, FLIGHT = 12, 4
LANES, HID_LANES, UP_ROWS, DOWN_AT = 128, 384, 344, 16
VMEM_LIMIT = 48 * 1024 * 1024
VMEM_MOST = 62 * 1024 * 1024


def place(routes):
    toks = routes.shape[1]
    rows = FLIGHT * PITCH
    slot = lax.broadcasted_iota(jnp.int32, (rows, toks), 0)
    expert = sum((slot >= PITCH * e).astype(jnp.int32) for e in range(1, FLIGHT))
    slot = slot - PITCH * expert
    first, second = routes[0:1] == expert, routes[1:2] == expert
    present = jnp.logical_or(first, second)
    earlier = lax.broadcasted_iota(jnp.int32, (toks, toks), 0) < lax.broadcasted_iota(jnp.int32, (toks, toks), 1)
    before = jnp.dot(
        present.astype(F32).astype(BF16), earlier.astype(F32).astype(BF16), preferred_element_type=F32
    )
    taken = jnp.logical_and(present, before == slot.astype(F32))
    return taken, first, second


def rescale(top):
    factor, power = jnp.ones_like(top), jnp.zeros_like(top)
    for bits in (32, 16, 8, 4, 2, 1):
        high = top * (2.0**-bits) >= 8192.0
        scale = jnp.where(high, 2.0**-bits, 1.0)
        top, factor = top * scale, factor * scale
        power = power - jnp.where(high, float(bits), 0.0)
    for bits in (32, 16, 8, 4, 2, 1):
        low = top * (2.0**bits) < 16384.0
        scale = jnp.where(low, 2.0**bits, 1.0)
        top, factor = top * scale, factor * scale
        power = power + jnp.where(low, float(bits), 0.0)
    return factor, power


def dispatch_kernel(routes_ref, tokens_ref, down_ref, out_ref):
    taken, _, _ = place(routes_ref[...])
    picked = jnp.dot(taken.astype(F32).astype(BF16), tokens_ref[...], preferred_element_type=F32)
    width = picked.shape[1]
    rows, total = down_ref.shape[1:]
    gap = jnp.zeros((DOWN_AT - PITCH, width), F32)
    for e in range(FLIGHT):
        mine = picked[e * PITCH : (e + 1) * PITCH]
        out_ref[e, :DOWN_AT] = jnp.concatenate([mine, gap], axis=0).astype(BF16)
        out_ref[e, DOWN_AT:, :total] = down_ref[e]
        out_ref[e, DOWN_AT:, total:] = jnp.zeros((rows, width - total), BF16)


def dispatch(routes_t, tokens, down):
    return pl.pallas_call(
        dispatch_kernel,
        out_shape=jax.ShapeDtypeStruct((FLIGHT, DOWN_AT + down.shape[1], tokens.shape[1]), BF16),
        compiler_params=pltpu.CompilerParams(vmem_limit_bytes=VMEM_LIMIT),
    )(routes_t, tokens, down)


def unpack_kernel(near_ref, rows_ref, down_ref):
    rows, total = near_ref.shape[1] - DOWN_AT, down_ref.shape[1]
    picked = [near_ref[e, :DOWN_AT].astype(F32)[:PITCH] for e in range(FLIGHT)]
    rows_ref[...] = jnp.concatenate(picked, axis=0).astype(BF16)
    down = [near_ref[e, DOWN_AT:, :total].astype(F32) for e in range(FLIGHT)]
    down_ref[...] = jnp.concatenate(down, axis=0).astype(BF16)


def unpack(near, total):
    flight, height, width = near.shape
    return pl.pallas_call(
        unpack_kernel,
        out_shape=(
            jax.ShapeDtypeStruct((flight * PITCH, width), BF16),
            jax.ShapeDtypeStruct((flight * (height - DOWN_AT), total), BF16),
        ),
        compiler_params=pltpu.CompilerParams(vmem_limit_bytes=VMEM_LIMIT),
    )(near)


def split_kernel(up_ref, out_ref):
    flight = up_ref.shape[0]
    units = out_ref.shape[2]
    blocks = out_ref.shape[0] // flight
    for e in range(flight):
        for b in range(blocks):
            out_ref[e * blocks + b] = up_ref[e, :, b * units : (b + 1) * units]


def split(up, units):
    flight, rows, total = up.shape
    return pl.pallas_call(
        split_kernel,
        out_shape=jax.ShapeDtypeStruct((flight * total // units, rows, units), BF16),
        compiler_params=pltpu.CompilerParams(vmem_limit_bytes=VMEM_LIMIT),
    )(up)


def prepare_kernel(mine_ref, got_ref, noise_ref, out_ref):
    owners, rows, units = got_ref.shape
    span = owners * rows
    got = got_ref[...].astype(F32).reshape(span, units).astype(BF16)
    same = lax.broadcasted_iota(jnp.int32, (span, span), 0) == lax.broadcasted_iota(jnp.int32, (span, span), 1)
    same = same.astype(F32).astype(BF16)
    up = lax.dot_general(got, same, (((0,), (0,)), ((), ())), preferred_element_type=F32)
    up = (up + noise_ref[...].astype(F32)).astype(BF16).astype(F32)
    top = jnp.max(jnp.max(jnp.abs(up), axis=1, keepdims=True), axis=0, keepdims=True)
    factor, power = rescale(top)
    power = jnp.broadcast_to(power, (out_ref.shape[0] - units, span))
    out_ref[...] = jnp.concatenate([up * factor, power], axis=0).astype(BF16)


def prepare(mine, got, noise_t):
    owners, rows, units = got.shape
    span = owners * rows
    return pl.pallas_call(
        prepare_kernel,
        grid_spec=pltpu.PrefetchScalarGridSpec(
            num_scalar_prefetch=1,
            grid=(1,),
            in_specs=[
                pl.BlockSpec((owners, rows, units), lambda i, m: (0, 0, 0)),
                pl.BlockSpec((units, span), lambda i, m: (0, m[0])),
            ],
            out_specs=pl.BlockSpec((UP_ROWS, span), lambda i, m: (0, 0)),
        ),
        out_shape=jax.ShapeDtypeStruct((UP_ROWS, span), BF16),
        compiler_params=pltpu.CompilerParams(vmem_limit_bytes=VMEM_LIMIT),
    )(mine, got, noise_t)


def up_kernel(x_hbm, w_hbm, out_ref, x_ref, w_ref, sems):
    chunks, group, units, span = w_ref.shape
    cols = group * span
    copies = []
    for c in range(chunks):
        copies.append(
            (
                pltpu.make_async_copy(x_hbm.at[:, c * cols : (c + 1) * cols], x_ref.at[c], sems.at[0, c]),
                pltpu.make_async_copy(w_hbm.at[c * group : (c + 1) * group], w_ref.at[c], sems.at[1, c]),
            )
        )
    for pair in copies:
        for copy in pair:
            copy.start()
    total = None
    for c, pair in enumerate(copies):
        for copy in pair:
            copy.wait()
        for g in range(group):
            x = x_ref[c, :, g * span : (g + 1) * span]
            term = lax.dot_general(x, w_ref[c, g], (((1,), (1,)), ((), ())), preferred_element_type=F32)
            total = term if total is None else total + term
    hidden = jnp.square(jnp.maximum(total, 0.0))
    factor, power = rescale(jnp.max(hidden, axis=1, keepdims=True))
    hidden = hidden.astype(BF16).astype(F32) * factor
    power = jnp.broadcast_to(power, (power.shape[0], out_ref.shape[1] - units))
    out_ref[...] = jnp.concatenate([hidden, power], axis=1).astype(BF16)


def up_project(x, w, chunks=4):
    rows, width = x.shape
    members, units, span = w.shape
    return pl.pallas_call(
        up_kernel,
        in_specs=[pl.BlockSpec(memory_space=pltpu.HBM)] * 2,
        out_shape=jax.ShapeDtypeStruct((rows, HID_LANES), BF16),
        scratch_shapes=[
            pltpu.VMEM((chunks, rows, width // chunks), BF16),
            pltpu.VMEM((chunks, members // chunks, units, span), BF16),
            pltpu.SemaphoreType.DMA((2, chunks)),
        ],
        compiler_params=pltpu.CompilerParams(vmem_limit_bytes=VMEM_MOST),
        cost_estimate=pl.CostEstimate(flops=2 * rows * width * units, bytes_accessed=2 * width * (rows + units), transcendentals=0),
    )(x, w)


def down_kernel(units, hid_hbm, w_hbm, out_ref, hid_ref, w_ref, sems):
    blocks = hid_ref.shape[0]
    chunks, cols, total = w_ref.shape
    first = [pltpu.make_async_copy(hid_hbm.at[b], hid_ref.at[b], sems.at[chunks + b]) for b in range(blocks)]
    copies = [pltpu.make_async_copy(w_hbm.at[c * cols : (c + 1) * cols], w_ref.at[c], sems.at[c]) for c in range(chunks)]
    for copy in first + copies:
        copy.start()
    hidden = []
    for b in range(blocks):
        first[b].wait()
        h = hid_ref[b].astype(F32)
        hidden.append(h[:, :units] * jnp.exp2(-h[:, units : units + 1]))
    hidden = jnp.concatenate(hidden, axis=1).astype(BF16)
    for c, copy in enumerate(copies):
        copy.wait()
        out = lax.dot_general(hidden, w_ref[c], (((1,), (1,)), ((), ())), preferred_element_type=F32)
        for z in range(blocks):
            for x in range(FLIGHT):
                top = (z * FLIGHT + x) * PITCH
                rows = out[top : top + PITCH]
                tiles = [rows[:, t : t + LANES] for t in range(0, cols, LANES)]
                at = c * PITCH * len(tiles)
                out_ref[x * blocks + z, at : at + PITCH * len(tiles)] = jnp.concatenate(tiles, axis=0).astype(BF16)


def down_project(hid, w, units, chunks=1):
    blocks, rows, lanes = hid.shape
    cols, total = w.shape
    return pl.pallas_call(
        lambda *r: down_kernel(units, *r),
        in_specs=[pl.BlockSpec(memory_space=pltpu.HBM)] * 2,
        out_shape=jax.ShapeDtypeStruct((rows // PITCH, PITCH * cols // LANES, LANES), BF16),
        scratch_shapes=[
            pltpu.VMEM((blocks, rows, lanes), BF16),
            pltpu.VMEM((chunks, cols // chunks, total), BF16),
            pltpu.SemaphoreType.DMA((chunks + blocks,)),
        ],
        compiler_params=pltpu.CompilerParams(vmem_limit_bytes=VMEM_MOST),
        cost_estimate=pl.CostEstimate(flops=2 * rows * cols * total, bytes_accessed=2 * cols * total + 2 * blocks * rows * lanes, transcendentals=0),
    )(hid, w)


def mix_kernel(rows, routes_ref, gates_ref, home_ref, out_ref):
    taken, first, second = place(routes_ref[...])
    gates = gates_ref[...]
    weight = jnp.where(first, gates[0:1], 0.0) + jnp.where(second, gates[1:2], 0.0)
    weight = jnp.where(taken, weight, 0.0)
    high = weight.astype(BF16)
    rest = weight - high.astype(F32)
    middle = rest.astype(BF16)
    low = (rest - middle.astype(F32)).astype(BF16)
    owners, height, _ = home_ref.shape
    blocks = owners // FLIGHT
    tiles = height // PITCH
    cols = tiles * LANES
    piece = cols // blocks
    home = []
    for b in range(blocks):
        each = []
        for e in range(FLIGHT):
            tall = home_ref[e * blocks + b].astype(F32)
            each.append(jnp.concatenate([tall[t * PITCH : (t + 1) * PITCH] for t in range(tiles)], axis=1))
        home.append(jnp.concatenate(each, axis=0))
    src = lax.broadcasted_iota(jnp.int32, (cols, cols), 0)
    dst = lax.broadcasted_iota(jnp.int32, (cols, cols), 1)
    block, group, row = src >> (piece.bit_length() - 1), (src & (piece - 1)) >> (rows.bit_length() - 1), src & (rows - 1)
    order = (dst == group * (blocks * rows) + block * rows + row).astype(F32).astype(BF16)
    turn = (((0,), (0,)), ((), ()))
    for q in range(blocks):
        chunk = jnp.concatenate([h[:, q * piece : (q + 1) * piece] for h in home], axis=1).astype(BF16)
        chunk = jnp.dot(chunk, order, preferred_element_type=F32).astype(BF16)
        total = None
        for part in (low, middle, high):
            term = lax.dot_general(part, chunk, turn, preferred_element_type=F32)
            total = term if total is None else total + term
        out_ref[:, q * cols : (q + 1) * cols] = total.astype(BF16)


def mix(routes_t, gates_t, home, rows):
    toks = routes_t.shape[1]
    owners, height, _ = home.shape
    width = owners // FLIGHT * height // PITCH * LANES
    return pl.pallas_call(
        lambda *r: mix_kernel(rows, *r),
        out_shape=jax.ShapeDtypeStruct((toks, width), BF16),
        compiler_params=pltpu.CompilerParams(vmem_limit_bytes=VMEM_LIMIT),
    )(routes_t, gates_t, home)


def on_device(tokens, routes, gate_values, dense_up, dense_down, up_noise):
    flight, rows, total = dense_up.shape
    units = up_noise.shape[1]
    blocks = total // units
    mine = lax.axis_index("y") * lax.axis_size("core") + lax.axis_index("core")

    near = lax.all_to_all(dispatch(routes.T, tokens, dense_down), "x", 0, 0, tiled=True)
    routed, down = unpack(near, total)
    everyone = lax.all_gather(routed, "z", axis=0, tiled=True)
    down = lax.all_gather(down, ("y", "core"), axis=0, tiled=True)

    pieces, _ = lax.optimization_barrier((split(dense_up, units), routed))
    got = lax.all_to_all(pieces, ("x", "z"), 0, 0, tiled=True)
    shard = prepare(mine.reshape(1), got, up_noise.T).astype(jnp.float16)
    up = lax.all_gather(shard, ("y", "core"))
    power = up[:, units : units + 1, :1].astype(F32)
    up = (up[:, :units].astype(F32) * jnp.exp2(-power)).astype(BF16)

    hidden = up_project(everyone, up).astype(jnp.float16)
    hidden = lax.all_gather(hidden, "z", axis=0, tiled=True).astype(BF16)
    out = down_project(hidden.reshape(blocks, -1, HID_LANES), down, units)
    home = lax.all_to_all(out, ("x", "z"), 0, 0, tiled=True)
    return mix(routes.T, gate_values.T, home, rows)


def solution(mesh):
    split = Mesh(mesh.devices.reshape(8, 2, 4, 8), ("y", "core", "x", "z"))
    every = ("y", "core", "x", "z")
    return jax.shard_map(
        on_device,
        mesh=split,
        in_specs=(
            P(every, None),
            P(every, None),
            P(every, None),
            P(None, every, None),
            P(None, every, None),
            P(None, ("x", "z")),
        ),
        out_specs=P(every, None),
        check_vma=False,
    )
```

```python
import jax, jax.numpy as jnp
from jax import lax
from jax.experimental import pallas as pl
from jax.experimental.pallas import tpu as pltpu
from jax.sharding import Mesh, PartitionSpec as P

F32, BF16 = jnp.float32, jnp.bfloat16
PITCH, FLIGHT = 12, 4
LANES, HID_LANES, UP_ROWS, SENT_ROWS = 128, 384, 344, 16
VMEM_LIMIT = 48 * 1024 * 1024
VMEM_MOST = 62 * 1024 * 1024


def place(routes):
    toks = routes.shape[1]
    rows = FLIGHT * PITCH
    slot = lax.broadcasted_iota(jnp.int32, (rows, toks), 0)
    expert = sum((slot >= PITCH * e).astype(jnp.int32) for e in range(1, FLIGHT))
    slot = slot - PITCH * expert
    first, second = routes[0:1] == expert, routes[1:2] == expert
    present = jnp.logical_or(first, second)
    earlier = lax.broadcasted_iota(jnp.int32, (toks, toks), 0) < lax.broadcasted_iota(jnp.int32, (toks, toks), 1)
    before = jnp.dot(
        present.astype(F32).astype(BF16), earlier.astype(F32).astype(BF16), preferred_element_type=F32
    )
    taken = jnp.logical_and(present, before == slot.astype(F32))
    return taken, first, second


def rescale(top):
    factor, power = jnp.ones_like(top), jnp.zeros_like(top)
    for bits in (32, 16, 8, 4, 2, 1):
        high = top * (2.0**-bits) >= 8192.0
        scale = jnp.where(high, 2.0**-bits, 1.0)
        top, factor = top * scale, factor * scale
        power = power - jnp.where(high, float(bits), 0.0)
    for bits in (32, 16, 8, 4, 2, 1):
        low = top * (2.0**bits) < 16384.0
        scale = jnp.where(low, 2.0**bits, 1.0)
        top, factor = top * scale, factor * scale
        power = power + jnp.where(low, float(bits), 0.0)
    return factor, power


def dispatch_kernel(routes_ref, tokens_ref, out_ref):
    taken, _, _ = place(routes_ref[...])
    picked = jnp.dot(taken.astype(F32).astype(BF16), tokens_ref[...], preferred_element_type=F32)
    width = out_ref.shape[2]
    rest = picked.shape[1] - width
    fold = width // rest
    for e in range(FLIGHT):
        mine = picked[e * PITCH : (e + 1) * PITCH]
        rows = [mine[:, :width]]
        for i in range(0, PITCH, fold):
            rows.append(jnp.concatenate([mine[i + k : i + k + 1, width:] for k in range(fold)], axis=1))
        out_ref[e] = jnp.concatenate(rows, axis=0).astype(BF16)


def dispatch(routes_t, tokens):
    return pl.pallas_call(
        dispatch_kernel,
        out_shape=jax.ShapeDtypeStruct((FLIGHT, SENT_ROWS, tokens.shape[1] * PITCH // SENT_ROWS), BF16),
        compiler_params=pltpu.CompilerParams(vmem_limit_bytes=VMEM_LIMIT),
    )(routes_t, tokens)


def unpack_kernel(near_ref, rows_ref):
    short = near_ref.shape[2]
    rest = rows_ref.shape[1] - short
    fold = short // rest
    rows = []
    for e in range(FLIGHT):
        sent = near_ref[e].astype(F32)
        tails = []
        for i in range(PITCH):
            at = PITCH + i // fold
            tails.append(sent[at : at + 1, i % fold * rest : (i % fold + 1) * rest])
        rows.append(jnp.concatenate([sent[:PITCH], jnp.concatenate(tails, axis=0)], axis=1))
    rows_ref[...] = jnp.concatenate(rows, axis=0).astype(BF16)


def unpack(near):
    flight, height, short = near.shape
    return pl.pallas_call(
        unpack_kernel,
        out_shape=jax.ShapeDtypeStruct((flight * PITCH, short * height // PITCH), BF16),
        compiler_params=pltpu.CompilerParams(vmem_limit_bytes=VMEM_LIMIT),
    )(near)


def split_kernel(up_ref, down_ref, out_ref):
    flight = up_ref.shape[0]
    units = out_ref.shape[2]
    blocks = out_ref.shape[0] // flight
    cuts = [slice(b * units, (b + 1) * units) for b in range(blocks)]
    for e in range(flight):
        down = down_ref[e].astype(F32)
        for b in range(blocks):
            row = jnp.concatenate([down[b : b + 1, cut] for cut in cuts], axis=0)
            out_ref[e * blocks + b] = jnp.concatenate([up_ref[e, :, cuts[b]].astype(F32), row], axis=0).astype(BF16)


def split(up, down, units):
    flight, rows, total = up.shape
    return pl.pallas_call(
        split_kernel,
        out_shape=jax.ShapeDtypeStruct((flight * total // units, 2 * rows, units), BF16),
        compiler_params=pltpu.CompilerParams(vmem_limit_bytes=VMEM_LIMIT),
    )(up, down)


def prepare_kernel(mine_ref, got_ref, noise_ref, out_ref, down_ref):
    owners, both, units = got_ref.shape
    rows = both // 2
    span = owners * rows
    got = got_ref[...].astype(F32)
    for b in range(rows):
        down_ref[:, b * units : (b + 1) * units] = got[:, rows + b, :].astype(BF16)
    flat = got[:, :rows].reshape(span, units).astype(BF16)
    same = lax.broadcasted_iota(jnp.int32, (span, span), 0) == lax.broadcasted_iota(jnp.int32, (span, span), 1)
    same = same.astype(F32).astype(BF16)
    up = lax.dot_general(flat, same, (((0,), (0,)), ((), ())), preferred_element_type=F32)
    up = (up + noise_ref[...].astype(F32)).astype(BF16).astype(F32)
    top = jnp.max(jnp.max(jnp.abs(up), axis=1, keepdims=True), axis=0, keepdims=True)
    factor, power = rescale(top)
    power = jnp.broadcast_to(power, (out_ref.shape[0] - units, span))
    out_ref[...] = jnp.concatenate([up * factor, power], axis=0).astype(BF16)


def prepare(mine, got, noise_t):
    owners, both, units = got.shape
    rows = both // 2
    span = owners * rows
    return pl.pallas_call(
        prepare_kernel,
        grid_spec=pltpu.PrefetchScalarGridSpec(
            num_scalar_prefetch=1,
            grid=(1,),
            in_specs=[
                pl.BlockSpec((owners, both, units), lambda i, m: (0, 0, 0)),
                pl.BlockSpec((units, span), lambda i, m: (0, m[0])),
            ],
            out_specs=(
                pl.BlockSpec((UP_ROWS, span), lambda i, m: (0, 0)),
                pl.BlockSpec((owners, rows * units), lambda i, m: (0, 0)),
            ),
        ),
        out_shape=(jax.ShapeDtypeStruct((UP_ROWS, span), BF16), jax.ShapeDtypeStruct((owners, rows * units), BF16)),
        compiler_params=pltpu.CompilerParams(vmem_limit_bytes=VMEM_LIMIT),
    )(mine, got, noise_t)


def up_kernel(x_hbm, w_hbm, out_ref, x_ref, w_ref, sems):
    chunks, group, units, span = w_ref.shape
    cols = group * span
    copies = []
    for c in range(chunks):
        copies.append(
            (
                pltpu.make_async_copy(x_hbm.at[:, c * cols : (c + 1) * cols], x_ref.at[c], sems.at[0, c]),
                pltpu.make_async_copy(w_hbm.at[c * group : (c + 1) * group], w_ref.at[c], sems.at[1, c]),
            )
        )
    for pair in copies:
        for copy in pair:
            copy.start()
    total = None
    for c, pair in enumerate(copies):
        for copy in pair:
            copy.wait()
        for g in range(group):
            x = x_ref[c, :, g * span : (g + 1) * span]
            term = lax.dot_general(x, w_ref[c, g], (((1,), (1,)), ((), ())), preferred_element_type=F32)
            total = term if total is None else total + term
    hidden = jnp.square(jnp.maximum(total, 0.0))
    factor, power = rescale(jnp.max(hidden, axis=1, keepdims=True))
    hidden = hidden.astype(BF16).astype(F32) * factor
    power = jnp.broadcast_to(power, (power.shape[0], out_ref.shape[1] - units))
    out_ref[...] = jnp.concatenate([hidden, power], axis=1).astype(BF16)


def up_project(x, w, chunks=4):
    rows, width = x.shape
    members, units, span = w.shape
    return pl.pallas_call(
        up_kernel,
        in_specs=[pl.BlockSpec(memory_space=pltpu.HBM)] * 2,
        out_shape=jax.ShapeDtypeStruct((rows, HID_LANES), BF16),
        scratch_shapes=[
            pltpu.VMEM((chunks, rows, width // chunks), BF16),
            pltpu.VMEM((chunks, members // chunks, units, span), BF16),
            pltpu.SemaphoreType.DMA((2, chunks)),
        ],
        compiler_params=pltpu.CompilerParams(vmem_limit_bytes=VMEM_MOST),
        cost_estimate=pl.CostEstimate(flops=2 * rows * width * units, bytes_accessed=2 * width * (rows + units), transcendentals=0),
    )(x, w)


def down_kernel(units, hid_hbm, w_hbm, out_ref, hid_ref, w_ref, sems):
    blocks = hid_ref.shape[0]
    chunks, cols, total = w_ref.shape
    first = [pltpu.make_async_copy(hid_hbm.at[b], hid_ref.at[b], sems.at[chunks + b]) for b in range(blocks)]
    copies = [pltpu.make_async_copy(w_hbm.at[c * cols : (c + 1) * cols], w_ref.at[c], sems.at[c]) for c in range(chunks)]
    for copy in first + copies:
        copy.start()
    hidden = []
    for b in range(blocks):
        first[b].wait()
        h = hid_ref[b].astype(F32)
        hidden.append(h[:, :units] * jnp.exp2(-h[:, units : units + 1]))
    hidden = jnp.concatenate(hidden, axis=1).astype(BF16)
    out = []
    for c, copy in enumerate(copies):
        copy.wait()
        out.append(lax.dot_general(hidden, w_ref[c], (((1,), (1,)), ((), ())), preferred_element_type=F32))
    out = jnp.concatenate(out, axis=1)
    for z in range(blocks):
        for x in range(FLIGHT):
            top = (z * FLIGHT + x) * PITCH
            tiles = [out[top : top + PITCH, t : t + LANES] for t in range(0, out.shape[1], LANES)]
            out_ref[x * blocks + z] = jnp.concatenate(tiles, axis=0).astype(BF16)


def down_project(hid, w, units, chunks=1):
    blocks, rows, lanes = hid.shape
    cols, total = w.shape
    return pl.pallas_call(
        lambda *r: down_kernel(units, *r),
        in_specs=[pl.BlockSpec(memory_space=pltpu.HBM)] * 2,
        out_shape=jax.ShapeDtypeStruct((rows // PITCH, PITCH * cols // LANES, LANES), BF16),
        scratch_shapes=[
            pltpu.VMEM((blocks, rows, lanes), BF16),
            pltpu.VMEM((chunks, cols // chunks, total), BF16),
            pltpu.SemaphoreType.DMA((chunks + blocks,)),
        ],
        compiler_params=pltpu.CompilerParams(vmem_limit_bytes=VMEM_MOST),
        cost_estimate=pl.CostEstimate(flops=2 * rows * cols * total, bytes_accessed=2 * cols * total + 2 * blocks * rows * lanes, transcendentals=0),
    )(hid, w)


def mix_kernel(routes_ref, gates_ref, home_ref, out_ref):
    taken, first, second = place(routes_ref[...])
    gates = gates_ref[...]
    weight = jnp.where(first, gates[0:1], 0.0) + jnp.where(second, gates[1:2], 0.0)
    weight = jnp.where(taken, weight, 0.0)
    high = weight.astype(BF16)
    rest = weight - high.astype(F32)
    middle = rest.astype(BF16)
    low = (rest - middle.astype(F32)).astype(BF16)
    owners, height, _ = home_ref.shape
    blocks = owners // FLIGHT
    tiles = height // PITCH
    cols = tiles * LANES
    piece = cols // blocks
    home = []
    for b in range(blocks):
        each = []
        for e in range(FLIGHT):
            tall = home_ref[e * blocks + b].astype(F32)
            each.append(jnp.concatenate([tall[t * PITCH : (t + 1) * PITCH] for t in range(tiles)], axis=1))
        home.append(jnp.concatenate(each, axis=0))
    src = lax.broadcasted_iota(jnp.int32, (cols, cols), 0)
    dst = lax.broadcasted_iota(jnp.int32, (cols, cols), 1)
    order = dst == (src & (piece - 1)) * blocks + (src >> (piece.bit_length() - 1))
    order = order.astype(F32).astype(BF16)
    turn = (((0,), (0,)), ((), ()))
    for q in range(blocks):
        chunk = jnp.concatenate([h[:, q * piece : (q + 1) * piece] for h in home], axis=1).astype(BF16)
        chunk = jnp.dot(chunk, order, preferred_element_type=F32).astype(BF16)
        total = None
        for part in (low, middle, high):
            term = lax.dot_general(part, chunk, turn, preferred_element_type=F32)
            total = term if total is None else total + term
        out_ref[:, q * cols : (q + 1) * cols] = total.astype(BF16)


def mix(routes_t, gates_t, home):
    toks = routes_t.shape[1]
    owners, height, _ = home.shape
    width = owners // FLIGHT * height // PITCH * LANES
    return pl.pallas_call(
        mix_kernel,
        out_shape=jax.ShapeDtypeStruct((toks, width), BF16),
        compiler_params=pltpu.CompilerParams(vmem_limit_bytes=VMEM_LIMIT),
    )(routes_t, gates_t, home)


def on_device(tokens, routes, gate_values, dense_up, dense_down, up_noise):
    flight, rows, total = dense_up.shape
    units = up_noise.shape[1]
    blocks = total // units
    mine = lax.axis_index("y") * lax.axis_size("core") + lax.axis_index("core")

    near = lax.all_to_all(dispatch(routes.T, tokens), "x", 0, 0, tiled=True)
    near, pieces = lax.optimization_barrier((near, split(dense_up, dense_down, units)))
    routed = unpack(near)
    everyone = lax.all_gather(routed, "z", axis=0, tiled=True)

    pieces, _ = lax.optimization_barrier((pieces, routed))
    got = lax.all_to_all(pieces, ("x", "z"), 0, 0, tiled=True)
    shard, down = prepare(mine.reshape(1), got, up_noise.T)
    down = lax.all_gather(down, ("y", "core"), axis=0, tiled=True)
    up = lax.all_gather(shard.astype(jnp.float16), ("y", "core"))
    power = up[:, units : units + 1, :1].astype(F32)
    up = (up[:, :units].astype(F32) * jnp.exp2(-power)).astype(BF16)

    hidden = up_project(everyone, up).astype(jnp.float16)
    hidden = lax.all_gather(hidden, "z", axis=0, tiled=True).astype(BF16)
    out = down_project(hidden.reshape(blocks, -1, HID_LANES), down, units)
    home = lax.all_to_all(out, ("x", "z"), 0, 0, tiled=True)
    return mix(routes.T, gate_values.T, home)


def solution(mesh):
    split = Mesh(mesh.devices.reshape(8, 2, 4, 8), ("y", "core", "x", "z"))
    every = ("y", "core", "x", "z")
    return jax.shard_map(
        on_device,
        mesh=split,
        in_specs=(
            P(every, None),
            P(every, None),
            P(every, None),
            P(None, every, None),
            P(None, every, None),
            P(None, ("x", "z")),
        ),
        out_specs=P(every, None),
        check_vma=False,
    )
```

```python
import jax, jax.numpy as jnp
from jax import lax
from jax.experimental import pallas as pl
from jax.experimental.pallas import tpu as pltpu
from jax.sharding import Mesh, PartitionSpec as P

F32, BF16 = jnp.float32, jnp.bfloat16
PITCH, FLIGHT = 12, 4
LANES, HID_LANES, UP_ROWS, SENT_ROWS = 128, 384, 344, 16
VMEM_LIMIT = 48 * 1024 * 1024
VMEM_MOST = 62 * 1024 * 1024


def place(routes):
    toks = routes.shape[1]
    rows = FLIGHT * PITCH
    slot = lax.broadcasted_iota(jnp.int32, (rows, toks), 0)
    expert = sum((slot >= PITCH * e).astype(jnp.int32) for e in range(1, FLIGHT))
    slot = slot - PITCH * expert
    first, second = routes[0:1] == expert, routes[1:2] == expert
    present = jnp.logical_or(first, second)
    earlier = lax.broadcasted_iota(jnp.int32, (toks, toks), 0) < lax.broadcasted_iota(jnp.int32, (toks, toks), 1)
    before = jnp.dot(
        present.astype(F32).astype(BF16), earlier.astype(F32).astype(BF16), preferred_element_type=F32
    )
    taken = jnp.logical_and(present, before == slot.astype(F32))
    return taken, first, second


def rescale(top):
    factor, power = jnp.ones_like(top), jnp.zeros_like(top)
    for bits in (32, 16, 8, 4, 2, 1):
        high = top * (2.0**-bits) >= 8192.0
        scale = jnp.where(high, 2.0**-bits, 1.0)
        top, factor = top * scale, factor * scale
        power = power - jnp.where(high, float(bits), 0.0)
    for bits in (32, 16, 8, 4, 2, 1):
        low = top * (2.0**bits) < 16384.0
        scale = jnp.where(low, 2.0**bits, 1.0)
        top, factor = top * scale, factor * scale
        power = power + jnp.where(low, float(bits), 0.0)
    return factor, power


def dispatch_kernel(routes_ref, tokens_hbm, out_ref, tokens_ref, sems):
    chunks, _, piece = tokens_ref.shape
    copies = [
        pltpu.make_async_copy(tokens_hbm.at[:, c * piece : (c + 1) * piece], tokens_ref.at[c], sems.at[c]) for c in range(chunks)
    ]
    for copy in copies[-1:] + copies[:-1]:
        copy.start()
    taken, _, _ = place(routes_ref[...])
    taken = taken.astype(F32).astype(BF16)

    def pick(c):
        copies[c].wait()
        return jnp.dot(taken, tokens_ref[c], preferred_element_type=F32)

    rest = pick(chunks - 1)
    for c in range(chunks - 1):
        picked = pick(c)
        for e in range(FLIGHT):
            at = e * PITCH
            tails = [rest[at + i : at + i + 1] for i in range(c, PITCH, chunks - 1)]
            rows = jnp.concatenate([picked[at : at + PITCH]] + tails, axis=0)
            out_ref[e, :, c * piece : (c + 1) * piece] = rows.astype(BF16)


def dispatch(routes_t, tokens):
    toks, width = tokens.shape
    chunks = SENT_ROWS // (SENT_ROWS - PITCH)
    piece = width // chunks
    return pl.pallas_call(
        dispatch_kernel,
        in_specs=[pl.BlockSpec(memory_space=pltpu.VMEM), pl.BlockSpec(memory_space=pltpu.HBM)],
        out_shape=jax.ShapeDtypeStruct((FLIGHT, SENT_ROWS, width - piece), BF16),
        scratch_shapes=[pltpu.VMEM((chunks, toks, piece), BF16), pltpu.SemaphoreType.DMA((chunks,))],
        compiler_params=pltpu.CompilerParams(vmem_limit_bytes=VMEM_MOST),
    )(routes_t, tokens)


def unpack_kernel(near_ref, rows_ref):
    short = near_ref.shape[2]
    rest = rows_ref.shape[1] - short
    fold = short // rest
    rows = []
    for e in range(FLIGHT):
        sent = near_ref[e].astype(F32)
        tails = []
        for i in range(PITCH):
            at = PITCH + i // fold
            tails.append(sent[at : at + 1, i % fold * rest : (i % fold + 1) * rest])
        rows.append(jnp.concatenate([sent[:PITCH], jnp.concatenate(tails, axis=0)], axis=1))
    rows_ref[...] = jnp.concatenate(rows, axis=0).astype(BF16)


def unpack(near):
    flight, height, short = near.shape
    return pl.pallas_call(
        unpack_kernel,
        out_shape=jax.ShapeDtypeStruct((flight * PITCH, short * height // PITCH), BF16),
        compiler_params=pltpu.CompilerParams(vmem_limit_bytes=VMEM_LIMIT),
    )(near)


def split_kernel(up_ref, down_ref, out_ref):
    flight = up_ref.shape[0]
    units = out_ref.shape[2]
    blocks = out_ref.shape[0] // flight
    cuts = [slice(b * units, (b + 1) * units) for b in range(blocks)]
    for e in range(flight):
        down = down_ref[e].astype(F32)
        for b in range(blocks):
            row = jnp.concatenate([down[b : b + 1, cut] for cut in cuts], axis=0)
            out_ref[e * blocks + b] = jnp.concatenate([up_ref[e, :, cuts[b]].astype(F32), row], axis=0).astype(BF16)


def split(up, down, units):
    flight, rows, total = up.shape
    return pl.pallas_call(
        split_kernel,
        out_shape=jax.ShapeDtypeStruct((flight * total // units, 2 * rows, units), BF16),
        compiler_params=pltpu.CompilerParams(vmem_limit_bytes=VMEM_LIMIT),
    )(up, down)


def prepare_kernel(mine_ref, got_ref, noise_ref, out_ref, down_ref):
    owners, both, units = got_ref.shape
    rows = both // 2
    span = owners * rows
    got = got_ref[...].astype(F32)
    for b in range(rows):
        down_ref[:, b * units : (b + 1) * units] = got[:, rows + b, :].astype(BF16)
    flat = got[:, :rows].reshape(span, units).astype(BF16)
    same = lax.broadcasted_iota(jnp.int32, (span, span), 0) == lax.broadcasted_iota(jnp.int32, (span, span), 1)
    same = same.astype(F32).astype(BF16)
    up = lax.dot_general(flat, same, (((0,), (0,)), ((), ())), preferred_element_type=F32)
    up = (up + noise_ref[...].astype(F32)).astype(BF16).astype(F32)
    top = jnp.max(jnp.max(jnp.abs(up), axis=1, keepdims=True), axis=0, keepdims=True)
    factor, power = rescale(top)
    power = jnp.broadcast_to(power, (out_ref.shape[0] - units, span))
    out_ref[...] = jnp.concatenate([up * factor, power], axis=0).astype(BF16)


def prepare(mine, got, noise_t):
    owners, both, units = got.shape
    rows = both // 2
    span = owners * rows
    return pl.pallas_call(
        prepare_kernel,
        grid_spec=pltpu.PrefetchScalarGridSpec(
            num_scalar_prefetch=1,
            grid=(1,),
            in_specs=[
                pl.BlockSpec((owners, both, units), lambda i, m: (0, 0, 0)),
                pl.BlockSpec((units, span), lambda i, m: (0, m[0])),
            ],
            out_specs=(
                pl.BlockSpec((UP_ROWS, span), lambda i, m: (0, 0)),
                pl.BlockSpec((owners, rows * units), lambda i, m: (0, 0)),
            ),
        ),
        out_shape=(jax.ShapeDtypeStruct((UP_ROWS, span), BF16), jax.ShapeDtypeStruct((owners, rows * units), BF16)),
        compiler_params=pltpu.CompilerParams(vmem_limit_bytes=VMEM_LIMIT),
    )(mine, got, noise_t)


def up_kernel(x_ref, w_ref, out_ref, acc_ref):
    step = pl.program_id(0)
    group, units, span = w_ref.shape
    total = None
    for g in range(group):
        x = x_ref[:, g * span : (g + 1) * span]
        term = lax.dot_general(x, w_ref[g], (((1,), (1,)), ((), ())), preferred_element_type=F32)
        total = term if total is None else total + term

    @pl.when(step == 0)
    def _():
        acc_ref[...] = total

    @pl.when(step > 0)
    def _():
        acc_ref[...] += total

    @pl.when(step == pl.num_programs(0) - 1)
    def _():
        hidden = jnp.square(jnp.maximum(acc_ref[...], 0.0))
        factor, power = rescale(jnp.max(hidden, axis=1, keepdims=True))
        hidden = hidden.astype(BF16).astype(F32) * factor
        power = jnp.broadcast_to(power, (power.shape[0], out_ref.shape[1] - units))
        out_ref[...] = jnp.concatenate([hidden, power], axis=1).astype(BF16)


def up_project(x, w, group=8):
    rows, width = x.shape
    members, units, span = w.shape
    return pl.pallas_call(
        up_kernel,
        grid=(members // group,),
        in_specs=[
            pl.BlockSpec((rows, group * span), lambda i: (0, i)),
            pl.BlockSpec((group, units, span), lambda i: (i, 0, 0)),
        ],
        out_specs=pl.BlockSpec((rows, HID_LANES), lambda i: (0, 0)),
        out_shape=jax.ShapeDtypeStruct((rows, HID_LANES), BF16),
        scratch_shapes=[pltpu.VMEM((rows, units), F32)],
        compiler_params=pltpu.CompilerParams(vmem_limit_bytes=VMEM_LIMIT),
        cost_estimate=pl.CostEstimate(flops=2 * rows * width * units, bytes_accessed=2 * width * (rows + units), transcendentals=0),
    )(x, w)


def join_kernel(units, hid_ref, out_ref):
    hidden = []
    for b in range(hid_ref.shape[0]):
        h = hid_ref[b].astype(F32)
        hidden.append(h[:, :units] * jnp.exp2(-h[:, units : units + 1]))
    out_ref[...] = jnp.concatenate(hidden, axis=1).astype(BF16)


def join(hid, units):
    blocks, rows, _ = hid.shape
    return pl.pallas_call(
        lambda *r: join_kernel(units, *r),
        out_shape=jax.ShapeDtypeStruct((rows, blocks * units), BF16),
        compiler_params=pltpu.CompilerParams(vmem_limit_bytes=VMEM_LIMIT),
    )(hid)


def down_kernel(hid_ref, w_ref, out_ref):
    out = lax.dot_general(hid_ref[...], w_ref[...], (((1,), (1,)), ((), ())), preferred_element_type=F32)
    blocks = out_ref.shape[0] // FLIGHT
    for z in range(blocks):
        for x in range(FLIGHT):
            top = (z * FLIGHT + x) * PITCH
            tiles = [out[top : top + PITCH, t : t + LANES] for t in range(0, out.shape[1], LANES)]
            out_ref[x * blocks + z] = jnp.concatenate(tiles, axis=0).astype(BF16)


def down_project(hid, w):
    rows, total = hid.shape
    cols = w.shape[0]
    return pl.pallas_call(
        down_kernel,
        out_shape=jax.ShapeDtypeStruct((rows // PITCH, PITCH * cols // LANES, LANES), BF16),
        compiler_params=pltpu.CompilerParams(vmem_limit_bytes=VMEM_LIMIT),
        cost_estimate=pl.CostEstimate(flops=2 * rows * cols * total, bytes_accessed=2 * total * (cols + rows), transcendentals=0),
    )(hid, w)


def mix_kernel(routes_ref, gates_ref, home_ref, out_ref):
    taken, first, second = place(routes_ref[...])
    gates = gates_ref[...]
    weight = jnp.where(first, gates[0:1], 0.0) + jnp.where(second, gates[1:2], 0.0)
    weight = jnp.where(taken, weight, 0.0)
    high = weight.astype(BF16)
    rest = weight - high.astype(F32)
    middle = rest.astype(BF16)
    low = rest - middle.astype(F32)
    weight = jnp.concatenate([low, middle.astype(F32), high.astype(F32)], axis=0).astype(BF16)
    owners, height, _ = home_ref.shape
    blocks = owners // FLIGHT
    tiles = height // PITCH
    cols = tiles * LANES
    piece = cols // blocks
    home = []
    for b in range(blocks):
        each = []
        for e in range(FLIGHT):
            tall = home_ref[e * blocks + b].astype(F32)
            each.append(jnp.concatenate([tall[t * PITCH : (t + 1) * PITCH] for t in range(tiles)], axis=1))
        home.append(jnp.concatenate(each, axis=0))
    src = lax.broadcasted_iota(jnp.int32, (cols, cols), 0)
    dst = lax.broadcasted_iota(jnp.int32, (cols, cols), 1)
    order = dst == (src & (piece - 1)) * blocks + (src >> (piece.bit_length() - 1))
    order = order.astype(F32).astype(BF16)
    chunks = [jnp.concatenate([h[:, q * piece : (q + 1) * piece] for h in home], axis=1) for q in range(blocks)]
    count = chunks[0].shape[0]
    chunks = jnp.dot(jnp.concatenate(chunks, axis=0).astype(BF16), order, preferred_element_type=F32).astype(BF16)
    for q in range(blocks):
        chunk = chunks[q * count : (q + 1) * count]
        total = lax.dot_general(
            weight, jnp.concatenate([chunk] * 3, axis=0), (((0,), (0,)), ((), ())), preferred_element_type=F32
        )
        out_ref[:, q * cols : (q + 1) * cols] = total.astype(BF16)


def mix(routes_t, gates_t, home):
    toks = routes_t.shape[1]
    owners, height, _ = home.shape
    width = owners // FLIGHT * height // PITCH * LANES
    return pl.pallas_call(
        mix_kernel,
        out_shape=jax.ShapeDtypeStruct((toks, width), BF16),
        compiler_params=pltpu.CompilerParams(vmem_limit_bytes=VMEM_LIMIT),
    )(routes_t, gates_t, home)


def on_device(tokens, routes, gate_values, dense_up, dense_down, up_noise):
    flight, rows, total = dense_up.shape
    units = up_noise.shape[1]
    blocks = total // units
    mine = lax.axis_index("y") * lax.axis_size("core") + lax.axis_index("core")

    near = lax.all_to_all(dispatch(routes.T, tokens), "x", 0, 0, tiled=True)
    near, pieces = lax.optimization_barrier((near, split(dense_up, dense_down, units)))
    routed = unpack(near)
    everyone = lax.all_gather(routed, "z", axis=0, tiled=True)

    pieces, _ = lax.optimization_barrier((pieces, routed))
    got = lax.all_to_all(pieces, ("x", "z"), 0, 0, tiled=True)
    shard, down = prepare(mine.reshape(1), got, up_noise.T)
    down = lax.all_gather(down, ("y", "core"), axis=0, tiled=True)
    up = lax.all_gather(shard.astype(jnp.float16), ("y", "core"))
    power = up[:, units : units + 1, :1].astype(F32)
    up = (up[:, :units].astype(F32) * jnp.exp2(-power)).astype(BF16)

    hidden = up_project(everyone, up).astype(jnp.float16)
    hidden = lax.all_gather(hidden, "z", axis=0, tiled=True).astype(BF16)
    hidden = join(hidden.reshape(blocks, -1, HID_LANES), units)
    out = down_project(hidden, down)
    home = lax.all_to_all(out, ("x", "z"), 0, 0, tiled=True)
    return mix(routes.T, gate_values.T, home)


def solution(mesh):
    split = Mesh(mesh.devices.reshape(8, 2, 4, 8), ("y", "core", "x", "z"))
    every = ("y", "core", "x", "z")
    return jax.shard_map(
        on_device,
        mesh=split,
        in_specs=(
            P(every, None),
            P(every, None),
            P(every, None),
            P(None, every, None),
            P(None, every, None),
            P(None, ("x", "z")),
        ),
        out_specs=P(every, None),
        check_vma=False,
    )
```

```python
import jax, jax.numpy as jnp
from jax import lax
from jax.experimental import pallas as pl
from jax.experimental.pallas import tpu as pltpu
from jax.sharding import Mesh, PartitionSpec as P

F32, BF16 = jnp.float32, jnp.bfloat16
PITCH, FLIGHT = 12, 4
LANES, HID_LANES, SENT_ROWS = 128, 384, 16
VMEM_LIMIT = 48 * 1024 * 1024
VMEM_SOME = 52_500_000


def place(routes):
    toks = routes.shape[1]
    rows = FLIGHT * PITCH
    slot = lax.broadcasted_iota(jnp.int32, (rows, toks), 0)
    expert = sum((slot >= PITCH * e).astype(jnp.int32) for e in range(1, FLIGHT))
    slot = slot - PITCH * expert
    first, second = routes[0:1] == expert, routes[1:2] == expert
    present = jnp.logical_or(first, second)
    earlier = lax.broadcasted_iota(jnp.int32, (toks, toks), 0) < lax.broadcasted_iota(jnp.int32, (toks, toks), 1)
    before = jnp.dot(
        present.astype(F32).astype(BF16), earlier.astype(F32).astype(BF16), preferred_element_type=F32
    )
    taken = jnp.logical_and(present, before == slot.astype(F32))
    return taken, first, second


def rescale(top):
    factor, power = jnp.ones_like(top), jnp.zeros_like(top)
    for bits in (32, 16, 8, 4, 2, 1):
        high = top * (2.0**-bits) >= 8192.0
        scale = jnp.where(high, 2.0**-bits, 1.0)
        top, factor = top * scale, factor * scale
        power = power - jnp.where(high, float(bits), 0.0)
    for bits in (32, 16, 8, 4, 2, 1):
        low = top * (2.0**bits) < 16384.0
        scale = jnp.where(low, 2.0**bits, 1.0)
        top, factor = top * scale, factor * scale
        power = power + jnp.where(low, float(bits), 0.0)
    return factor, power


def dispatch_kernel(routes_ref, tokens_hbm, out_ref, shrink_ref, tokens_ref, sems):
    chunks, _, piece = tokens_ref.shape
    copies = [
        pltpu.make_async_copy(tokens_hbm.at[:, c * piece : (c + 1) * piece], tokens_ref.at[c], sems.at[c]) for c in range(chunks)
    ]
    for copy in copies:
        copy.start()
    taken, _, _ = place(routes_ref[...])
    taken = taken.astype(F32).astype(BF16)
    picked, top = [], None
    for c in range(chunks):
        copies[c].wait()
        picked.append(jnp.dot(taken, tokens_ref[c], preferred_element_type=F32))
        most = jnp.max(jnp.abs(picked[c]), axis=1, keepdims=True)
        top = most if top is None else jnp.maximum(top, most)
    grow, _ = rescale(top)
    shrink_ref[...] = 1.0 / grow
    rest = picked[-1] * grow
    for c in range(chunks - 1):
        rows = picked[c] * grow
        for e in range(FLIGHT):
            at = e * PITCH
            tails = [rest[at + i : at + i + 1] for i in range(c, PITCH, chunks - 1)]
            out_ref[e, :, c * piece : (c + 1) * piece] = jnp.concatenate([rows[at : at + PITCH]] + tails, axis=0).astype(BF16)


def dispatch(routes_t, tokens):
    toks, width = tokens.shape
    chunks = SENT_ROWS // (SENT_ROWS - PITCH)
    piece = width // chunks
    return pl.pallas_call(
        dispatch_kernel,
        in_specs=[pl.BlockSpec(memory_space=pltpu.VMEM), pl.BlockSpec(memory_space=pltpu.HBM)],
        out_shape=(
            jax.ShapeDtypeStruct((FLIGHT, SENT_ROWS, width - piece), BF16),
            jax.ShapeDtypeStruct((FLIGHT * PITCH, 1), F32),
        ),
        scratch_shapes=[pltpu.VMEM((chunks, toks, piece), BF16), pltpu.SemaphoreType.DMA((chunks,))],
        compiler_params=pltpu.CompilerParams(vmem_limit_bytes=VMEM_LIMIT),
    )(routes_t, tokens)


def unpack_kernel(here_ref, *refs):
    near, rows_ref = refs[:-1], refs[-1]
    here = here_ref[0]
    short = near[0].shape[1]
    rest = rows_ref.shape[1] - short
    fold = short // rest
    blocks = [ref[...].astype(F32) for ref in near]
    rows = []
    for k in range(FLIGHT):
        sent = blocks[(FLIGHT - 1 - k) % FLIGHT]
        for x in range(FLIGHT - 1):
            sent = jnp.where(here == x, blocks[(x - k) % FLIGHT], sent)
        tails = []
        for i in range(PITCH):
            at = PITCH + i // fold
            tails.append(sent[at : at + 1, i % fold * rest : (i % fold + 1) * rest])
        rows.append(jnp.concatenate([sent[:PITCH], jnp.concatenate(tails, axis=0)], axis=1))
    rows_ref[...] = jnp.concatenate(rows, axis=0).astype(BF16)


def unpack(here, near):
    height, short = near[0].shape
    width = short * height // PITCH
    whole = pl.BlockSpec((height, short), lambda i, m: (0, 0))
    return pl.pallas_call(
        unpack_kernel,
        grid_spec=pltpu.PrefetchScalarGridSpec(
            num_scalar_prefetch=1,
            grid=(1,),
            in_specs=[whole] * len(near),
            out_specs=pl.BlockSpec((len(near) * PITCH, width), lambda i, m: (0, 0)),
        ),
        out_shape=jax.ShapeDtypeStruct((len(near) * PITCH, width), BF16),
        compiler_params=pltpu.CompilerParams(vmem_limit_bytes=VMEM_LIMIT),
    )(here, *near)


def split_kernel(up_ref, down_ref, out_ref):
    flight, rows, total = up_ref.shape
    wide = out_ref.shape[2]
    blocks = out_ref.shape[0] // flight
    units = total // blocks
    rim = jnp.zeros((rows, wide - units), F32)
    fill = jnp.zeros((rows - total // wide, wide), F32)
    for e in range(flight):
        up, down = up_ref[e].astype(F32), down_ref[e].astype(F32)
        for b in range(blocks):
            top = jnp.concatenate([up[:, b * units : (b + 1) * units], rim], axis=1)
            row = [down[b : b + 1, at : at + wide] for at in range(0, total, wide)]
            out_ref[e * blocks + b] = jnp.concatenate([top] + row + [fill], axis=0).astype(BF16)


def split(up, down, blocks):
    flight, rows, _ = up.shape
    return pl.pallas_call(
        split_kernel,
        out_shape=jax.ShapeDtypeStruct((flight * blocks, 2 * rows, HID_LANES), BF16),
        compiler_params=pltpu.CompilerParams(vmem_limit_bytes=VMEM_LIMIT),
    )(up, down)


def prepare_kernel(mine_ref, got_ref, noise_ref, out_ref):
    owners, both, wide = got_ref.shape
    rows = both // 2
    units, span = noise_ref.shape
    got = got_ref[...].astype(F32)
    flat = got[:, :rows, :units].reshape(span, units).astype(BF16)
    same = lax.broadcasted_iota(jnp.int32, (span, span), 0) == lax.broadcasted_iota(jnp.int32, (span, span), 1)
    same = same.astype(F32).astype(BF16)
    up = lax.dot_general(flat, same, (((0,), (0,)), ((), ())), preferred_element_type=F32)
    up = (up + noise_ref[...].astype(F32)).astype(BF16)
    for half in range(span // LANES):
        out_ref[half * units : (half + 1) * units] = up[:, half * LANES : (half + 1) * LANES]
    start = span // LANES * units
    per = wide // LANES
    for q in range((out_ref.shape[0] - start) // owners):
        row = got[:, rows + q // per, q % per * LANES : (q % per + 1) * LANES]
        out_ref[start + q * owners : start + (q + 1) * owners] = row.astype(BF16)


def prepare(mine, got, noise_t, total):
    owners, both, wide = got.shape
    units = noise_t.shape[0]
    span = owners * both // 2
    height = (span * units + owners * total) // LANES
    return pl.pallas_call(
        prepare_kernel,
        grid_spec=pltpu.PrefetchScalarGridSpec(
            num_scalar_prefetch=1,
            grid=(1,),
            in_specs=[
                pl.BlockSpec((owners, both, wide), lambda i, m: (0, 0, 0)),
                pl.BlockSpec((units, span), lambda i, m: (0, m[0])),
            ],
            out_specs=pl.BlockSpec((height, LANES), lambda i, m: (0, 0)),
        ),
        out_shape=jax.ShapeDtypeStruct((height, LANES), BF16),
        compiler_params=pltpu.CompilerParams(vmem_limit_bytes=VMEM_LIMIT),
    )(mine, got, noise_t)


def up_kernel(x_ref, w_ref, out_ref, acc_ref):
    step = pl.program_id(0)
    group, height, _ = w_ref.shape
    units = acc_ref.shape[1]
    parts = height // units
    span = parts * LANES
    total = None
    for g in range(group):
        w = jnp.concatenate([w_ref[g, h * units : (h + 1) * units] for h in range(parts)], axis=1)
        x = x_ref[:, g * span : (g + 1) * span]
        term = lax.dot_general(x, w, (((1,), (1,)), ((), ())), preferred_element_type=F32)
        total = term if total is None else total + term

    @pl.when(step == 0)
    def _():
        acc_ref[...] = total

    @pl.when(step > 0)
    def _():
        acc_ref[...] += total

    @pl.when(step == pl.num_programs(0) - 1)
    def _():
        hidden = jnp.square(jnp.maximum(acc_ref[...], 0.0))
        factor, power = rescale(jnp.max(hidden, axis=1, keepdims=True))
        hidden = hidden.astype(BF16).astype(F32) * factor
        power = jnp.broadcast_to(power, (power.shape[0], out_ref.shape[1] - units))
        out_ref[...] = jnp.concatenate([hidden, power], axis=1).astype(BF16)


def up_project(x, w, units, group=8):
    rows, width = x.shape
    members = w.shape[0]
    span = width // members
    height = span // LANES * units
    return pl.pallas_call(
        up_kernel,
        grid=(members // group,),
        in_specs=[
            pl.BlockSpec((rows, group * span), lambda i: (0, i)),
            pl.BlockSpec((group, height, LANES), lambda i: (i, 0, 0)),
        ],
        out_specs=pl.BlockSpec((rows, HID_LANES), lambda i: (0, 0)),
        out_shape=jax.ShapeDtypeStruct((rows, HID_LANES), BF16),
        scratch_shapes=[pltpu.VMEM((rows, units), F32)],
        compiler_params=pltpu.CompilerParams(vmem_limit_bytes=VMEM_SOME),
        cost_estimate=pl.CostEstimate(flops=2 * rows * width * units, bytes_accessed=2 * width * (rows + units), transcendentals=0),
    )(x, w)


def join_kernel(units, hid_ref, out_ref):
    hidden = []
    for b in range(hid_ref.shape[0]):
        h = hid_ref[b].astype(F32)
        hidden.append(h[:, :units] * jnp.exp2(-h[:, units : units + 1]))
    out_ref[...] = jnp.concatenate(hidden, axis=1).astype(BF16)


def join(hid, units):
    blocks, rows, _ = hid.shape
    return pl.pallas_call(
        lambda *r: join_kernel(units, *r),
        out_shape=jax.ShapeDtypeStruct((rows, blocks * units), BF16),
        compiler_params=pltpu.CompilerParams(vmem_limit_bytes=VMEM_LIMIT),
    )(hid)


def down_kernel(hid_ref, w_ref, out_ref):
    members, height, _ = w_ref.shape
    tiles = hid_ref.shape[1] // LANES
    count = height // tiles
    w = [w_ref[:, q * count : (q + 1) * count].reshape(members * count, LANES) for q in range(tiles)]
    w = jnp.concatenate(w, axis=1)
    out = lax.dot_general(hid_ref[...], w, (((1,), (1,)), ((), ())), preferred_element_type=F32)
    blocks = out_ref.shape[0] // FLIGHT
    for z in range(blocks):
        for x in range(FLIGHT):
            top = (z * FLIGHT + x) * PITCH
            tiles = [out[top : top + PITCH, t : t + LANES] for t in range(0, out.shape[1], LANES)]
            out_ref[x * blocks + z] = jnp.concatenate(tiles, axis=0).astype(BF16)


def down_project(hid, w):
    rows, total = hid.shape
    members, height, _ = w.shape
    cols = members * height // 2 * LANES // total
    return pl.pallas_call(
        down_kernel,
        grid=(1,),
        in_specs=[
            pl.BlockSpec((rows, total), lambda i: (0, 0)),
            pl.BlockSpec((members, height // 2, LANES), lambda i: (0, 1, 0)),
        ],
        out_specs=pl.BlockSpec((rows // PITCH, PITCH * cols // LANES, LANES), lambda i: (0, 0, 0)),
        out_shape=jax.ShapeDtypeStruct((rows // PITCH, PITCH * cols // LANES, LANES), BF16),
        compiler_params=pltpu.CompilerParams(vmem_limit_bytes=VMEM_SOME),
        cost_estimate=pl.CostEstimate(flops=2 * rows * cols * total, bytes_accessed=2 * total * (cols + rows), transcendentals=0),
    )(hid, w)


def mix_kernel(routes_ref, gates_ref, shrink_ref, home_ref, out_ref):
    taken, first, second = place(routes_ref[...])
    gates = gates_ref[...]
    weight = jnp.where(first, gates[0:1], 0.0) + jnp.where(second, gates[1:2], 0.0)
    weight = jnp.where(taken, weight, 0.0) * shrink_ref[...]
    high = weight.astype(BF16)
    rest = weight - high.astype(F32)
    middle = rest.astype(BF16)
    low = rest - middle.astype(F32)
    weight = jnp.concatenate([low, middle.astype(F32), high.astype(F32)], axis=0).astype(BF16)
    owners, height, _ = home_ref.shape
    blocks = owners // FLIGHT
    tiles = height // PITCH
    cols = tiles * LANES
    piece = cols // blocks
    home = []
    for b in range(blocks):
        each = []
        for e in range(FLIGHT):
            tall = home_ref[e * blocks + b].astype(F32)
            each.append(jnp.concatenate([tall[t * PITCH : (t + 1) * PITCH] for t in range(tiles)], axis=1))
        home.append(jnp.concatenate(each, axis=0) * shrink_ref[...])
    src = lax.broadcasted_iota(jnp.int32, (cols, cols), 0)
    dst = lax.broadcasted_iota(jnp.int32, (cols, cols), 1)
    order = dst == (src & (piece - 1)) * blocks + (src >> (piece.bit_length() - 1))
    order = order.astype(F32).astype(BF16)
    chunks = [jnp.concatenate([h[:, q * piece : (q + 1) * piece] for h in home], axis=1) for q in range(blocks)]
    count = chunks[0].shape[0]
    chunks = jnp.dot(jnp.concatenate(chunks, axis=0).astype(BF16), order, preferred_element_type=F32).astype(BF16)
    for q in range(blocks):
        chunk = chunks[q * count : (q + 1) * count]
        total = lax.dot_general(
            weight, jnp.concatenate([chunk] * 3, axis=0), (((0,), (0,)), ((), ())), preferred_element_type=F32
        )
        out_ref[:, q * cols : (q + 1) * cols] = total.astype(BF16)


def mix(routes_t, gates_t, shrink, home):
    toks = routes_t.shape[1]
    owners, height, _ = home.shape
    width = owners // FLIGHT * height // PITCH * LANES
    return pl.pallas_call(
        mix_kernel,
        out_shape=jax.ShapeDtypeStruct((toks, width), BF16),
        compiler_params=pltpu.CompilerParams(vmem_limit_bytes=VMEM_LIMIT),
    )(routes_t, gates_t, shrink, home)


def on_device(tokens, routes, gate_values, dense_up, dense_down, up_noise):
    flight, _, total = dense_up.shape
    units = up_noise.shape[1]
    blocks = total // units
    here = lax.axis_index("x")
    mine = lax.axis_index("y") * lax.axis_size("core") + lax.axis_index("core")

    got = lax.all_to_all(split(dense_up, dense_down, blocks), ("x", "z"), 0, 0, tiled=True)

    outgoing, shrink = dispatch(routes.T, tokens)
    near = []
    for s in range(flight):
        block = lax.dynamic_index_in_dim(outgoing, (here + s) % flight, 0, keepdims=False)
        near.append(lax.ppermute(block, "x", [(i, (i + s) % flight) for i in range(flight)]) if s else block)
    got, near[1], near[2] = lax.optimization_barrier((got, near[1], near[2]))
    shard = prepare(mine.reshape(1), got, up_noise.T, total)
    weights = lax.all_gather(shard, ("y", "core"))
    routed = unpack(here.reshape(1), near).astype(jnp.float16)
    routed, _ = lax.optimization_barrier((routed, shard))
    everyone = lax.all_gather(routed, "z", axis=0, tiled=True).astype(BF16)

    hidden = up_project(everyone, weights, units).astype(jnp.float16)
    hidden = lax.all_gather(hidden, "z", axis=0, tiled=True).astype(BF16)
    hidden = join(hidden.reshape(blocks, -1, HID_LANES), units)
    out = down_project(hidden, weights)
    home = lax.all_to_all(out, ("x", "z"), 0, 0, tiled=True)
    return mix(routes.T, gate_values.T, shrink, home)


def solution(mesh):
    split = Mesh(mesh.devices.reshape(8, 2, 4, 8), ("y", "core", "x", "z"))
    every = ("y", "core", "x", "z")
    return jax.shard_map(
        on_device,
        mesh=split,
        in_specs=(
            P(every, None),
            P(every, None),
            P(every, None),
            P(None, every, None),
            P(None, every, None),
            P(None, ("x", "z")),
        ),
        out_specs=P(every, None),
        check_vma=False,
    )
```

```python
import jax, jax.numpy as jnp
from jax import lax
from jax.experimental import pallas as pl
from jax.experimental.pallas import tpu as pltpu
from jax.sharding import Mesh, PartitionSpec as P

F32, BF16 = jnp.float32, jnp.bfloat16
PITCH, FLIGHT = 12, 4
LANES, HID_LANES, SENT_ROWS = 128, 384, 16
VMEM_LIMIT = 48 * 1024 * 1024
VMEM_SOME = 48_500_000


def place(routes):
    toks = routes.shape[1]
    rows = FLIGHT * PITCH
    slot = lax.broadcasted_iota(jnp.int32, (rows, toks), 0)
    expert = sum((slot >= PITCH * e).astype(jnp.int32) for e in range(1, FLIGHT))
    slot = slot - PITCH * expert
    first, second = routes[0:1] == expert, routes[1:2] == expert
    present = jnp.logical_or(first, second)
    earlier = lax.broadcasted_iota(jnp.int32, (toks, toks), 0) < lax.broadcasted_iota(jnp.int32, (toks, toks), 1)
    before = jnp.dot(
        present.astype(F32).astype(BF16), earlier.astype(F32).astype(BF16), preferred_element_type=F32
    )
    taken = jnp.logical_and(present, before == slot.astype(F32))
    return taken, first, second


def rescale(top):
    factor, power = jnp.ones_like(top), jnp.zeros_like(top)
    for bits in (32, 16, 8, 4, 2, 1):
        high = top * (2.0**-bits) >= 8192.0
        scale = jnp.where(high, 2.0**-bits, 1.0)
        top, factor = top * scale, factor * scale
        power = power - jnp.where(high, float(bits), 0.0)
    for bits in (32, 16, 8, 4, 2, 1):
        low = top * (2.0**bits) < 16384.0
        scale = jnp.where(low, 2.0**bits, 1.0)
        top, factor = top * scale, factor * scale
        power = power + jnp.where(low, float(bits), 0.0)
    return factor, power


def dispatch_kernel(routes_ref, tokens_hbm, out_ref, shrink_ref, tokens_ref, sems):
    chunks, _, piece = tokens_ref.shape
    copies = [
        pltpu.make_async_copy(tokens_hbm.at[:, c * piece : (c + 1) * piece], tokens_ref.at[c], sems.at[c]) for c in range(chunks)
    ]
    for copy in copies:
        copy.start()
    taken, _, _ = place(routes_ref[...])
    taken = taken.astype(F32).astype(BF16)
    picked, top = [], None
    for c in range(chunks):
        copies[c].wait()
        picked.append(jnp.dot(taken, tokens_ref[c], preferred_element_type=F32))
        most = jnp.max(jnp.abs(picked[c]), axis=1, keepdims=True)
        top = most if top is None else jnp.maximum(top, most)
    grow, _ = rescale(top)
    shrink_ref[...] = 1.0 / grow
    rest = picked[-1] * grow
    for c in range(chunks - 1):
        rows = picked[c] * grow
        for e in range(FLIGHT):
            at = e * PITCH
            tails = [rest[at + i : at + i + 1] for i in range(c, PITCH, chunks - 1)]
            out_ref[e, :, c * piece : (c + 1) * piece] = jnp.concatenate([rows[at : at + PITCH]] + tails, axis=0).astype(BF16)


def dispatch(routes_t, tokens):
    toks, width = tokens.shape
    chunks = SENT_ROWS // (SENT_ROWS - PITCH)
    piece = width // chunks
    return pl.pallas_call(
        dispatch_kernel,
        in_specs=[pl.BlockSpec(memory_space=pltpu.VMEM), pl.BlockSpec(memory_space=pltpu.HBM)],
        out_shape=(
            jax.ShapeDtypeStruct((FLIGHT, SENT_ROWS, width - piece), BF16),
            jax.ShapeDtypeStruct((FLIGHT * PITCH, 1), F32),
        ),
        scratch_shapes=[pltpu.VMEM((chunks, toks, piece), BF16), pltpu.SemaphoreType.DMA((chunks,))],
        compiler_params=pltpu.CompilerParams(vmem_limit_bytes=VMEM_LIMIT),
    )(routes_t, tokens)


def unpack_kernel(here_ref, *refs):
    near, rows_ref = refs[:-1], refs[-1]
    here = here_ref[0]
    short = near[0].shape[1]
    rest = rows_ref.shape[1] - short
    fold = short // rest
    blocks = [ref[...].astype(F32) for ref in near]
    rows = []
    for k in range(FLIGHT):
        sent = blocks[(FLIGHT - 1 - k) % FLIGHT]
        for x in range(FLIGHT - 1):
            sent = jnp.where(here == x, blocks[(x - k) % FLIGHT], sent)
        tails = []
        for i in range(PITCH):
            at = PITCH + i // fold
            tails.append(sent[at : at + 1, i % fold * rest : (i % fold + 1) * rest])
        rows.append(jnp.concatenate([sent[:PITCH], jnp.concatenate(tails, axis=0)], axis=1))
    rows_ref[...] = jnp.concatenate(rows, axis=0).astype(BF16)


def unpack(here, near):
    height, short = near[0].shape
    width = short * height // PITCH
    whole = pl.BlockSpec((height, short), lambda i, m: (0, 0))
    return pl.pallas_call(
        unpack_kernel,
        grid_spec=pltpu.PrefetchScalarGridSpec(
            num_scalar_prefetch=1,
            grid=(1,),
            in_specs=[whole] * len(near),
            out_specs=pl.BlockSpec((len(near) * PITCH, width), lambda i, m: (0, 0)),
        ),
        out_shape=jax.ShapeDtypeStruct((len(near) * PITCH, width), BF16),
        compiler_params=pltpu.CompilerParams(vmem_limit_bytes=VMEM_LIMIT),
    )(here, *near)


def split_kernel(up_ref, down_ref, out_ref):
    flight, rows, total = up_ref.shape
    wide = out_ref.shape[2]
    blocks = out_ref.shape[0] // flight
    units = total // blocks
    rim = jnp.zeros((rows, wide - units), F32)
    fill = jnp.zeros((rows - total // wide, wide), F32)
    for e in range(flight):
        up, down = up_ref[e].astype(F32), down_ref[e].astype(F32)
        for b in range(blocks):
            top = jnp.concatenate([up[:, b * units : (b + 1) * units], rim], axis=1)
            row = [down[b : b + 1, at : at + wide] for at in range(0, total, wide)]
            out_ref[e * blocks + b] = jnp.concatenate([top] + row + [fill], axis=0).astype(BF16)


def split(up, down, blocks):
    flight, rows, _ = up.shape
    return pl.pallas_call(
        split_kernel,
        out_shape=jax.ShapeDtypeStruct((flight * blocks, 2 * rows, HID_LANES), BF16),
        compiler_params=pltpu.CompilerParams(vmem_limit_bytes=VMEM_LIMIT),
    )(up, down)


def prepare_kernel(mine_ref, got_ref, noise_ref, out_ref):
    owners, both, wide = got_ref.shape
    rows = both // 2
    units, span = noise_ref.shape
    got = got_ref[...].astype(F32)
    flat = got[:, :rows, :units].reshape(span, units).astype(BF16)
    same = lax.broadcasted_iota(jnp.int32, (span, span), 0) == lax.broadcasted_iota(jnp.int32, (span, span), 1)
    same = same.astype(F32).astype(BF16)
    up = lax.dot_general(flat, same, (((0,), (0,)), ((), ())), preferred_element_type=F32)
    up = (up + noise_ref[...].astype(F32)).astype(BF16)
    for half in range(span // LANES):
        out_ref[half * units : (half + 1) * units] = up[:, half * LANES : (half + 1) * LANES]
    start = span // LANES * units
    per = wide // LANES
    for q in range((out_ref.shape[0] - start) // owners):
        row = got[:, rows + q // per, q % per * LANES : (q % per + 1) * LANES]
        out_ref[start + q * owners : start + (q + 1) * owners] = row.astype(BF16)


def prepare(mine, got, noise_t, total):
    owners, both, wide = got.shape
    units = noise_t.shape[0]
    span = owners * both // 2
    height = (span * units + owners * total) // LANES
    return pl.pallas_call(
        prepare_kernel,
        grid_spec=pltpu.PrefetchScalarGridSpec(
            num_scalar_prefetch=1,
            grid=(1,),
            in_specs=[
                pl.BlockSpec((owners, both, wide), lambda i, m: (0, 0, 0)),
                pl.BlockSpec((units, span), lambda i, m: (0, m[0])),
            ],
            out_specs=pl.BlockSpec((height, LANES), lambda i, m: (0, 0)),
        ),
        out_shape=jax.ShapeDtypeStruct((height, LANES), BF16),
        compiler_params=pltpu.CompilerParams(vmem_limit_bytes=VMEM_LIMIT),
    )(mine, got, noise_t)


def up_kernel(x_ref, w_hbm, out_ref, down_ref, w_ref, sems):
    members, height, _ = w_ref.shape
    chunks = sems.shape[0] - 1
    group = members // chunks
    units = height * LANES * members // x_ref.shape[1]
    parts = height // units
    span = parts * LANES
    copies = []
    for c in range(chunks):
        some = slice(c * group, (c + 1) * group)
        copies.append(pltpu.make_async_copy(w_hbm.at[some, :height], w_ref.at[some], sems.at[c]))
    later = pltpu.make_async_copy(w_hbm.at[:, height:], down_ref, sems.at[chunks])
    for copy in copies + [later]:
        copy.start()
    total = None
    for g in range(members):
        if g % group == 0:
            copies[g // group].wait()
        w = jnp.concatenate([w_ref[g, h * units : (h + 1) * units] for h in range(parts)], axis=1)
        x = x_ref[:, g * span : (g + 1) * span]
        term = lax.dot_general(x, w, (((1,), (1,)), ((), ())), preferred_element_type=F32)
        total = term if total is None else total + term
    hidden = jnp.square(jnp.maximum(total, 0.0))
    factor, power = rescale(jnp.max(hidden, axis=1, keepdims=True))
    hidden = hidden.astype(BF16).astype(F32) * factor
    power = jnp.broadcast_to(power, (power.shape[0], out_ref.shape[1] - units))
    out_ref[...] = jnp.concatenate([hidden, power], axis=1).astype(BF16)
    later.wait()


def up_project(x, w, units, chunks=4):
    rows, width = x.shape
    members, both, _ = w.shape
    height = width // members // LANES * units
    return pl.pallas_call(
        up_kernel,
        in_specs=[pl.BlockSpec(memory_space=pltpu.VMEM), pl.BlockSpec(memory_space=pltpu.HBM)],
        out_specs=(pl.BlockSpec(memory_space=pltpu.VMEM), pl.BlockSpec(memory_space=pltpu.VMEM)),
        out_shape=(
            jax.ShapeDtypeStruct((rows, HID_LANES), BF16),
            jax.ShapeDtypeStruct((members, both - height, LANES), BF16),
        ),
        scratch_shapes=[pltpu.VMEM((members, height, LANES), BF16), pltpu.SemaphoreType.DMA((chunks + 1,))],
        compiler_params=pltpu.CompilerParams(vmem_limit_bytes=VMEM_SOME),
        cost_estimate=pl.CostEstimate(flops=2 * rows * width * units, bytes_accessed=2 * width * (rows + units), transcendentals=0),
    )(x, w)


def join_kernel(units, hid_ref, out_ref):
    hidden = []
    for b in range(hid_ref.shape[0]):
        h = hid_ref[b].astype(F32)
        hidden.append(h[:, :units] * jnp.exp2(-h[:, units : units + 1]))
    out_ref[...] = jnp.concatenate(hidden, axis=1).astype(BF16)


def join(hid, units):
    blocks, rows, _ = hid.shape
    return pl.pallas_call(
        lambda *r: join_kernel(units, *r),
        out_shape=jax.ShapeDtypeStruct((rows, blocks * units), BF16),
        compiler_params=pltpu.CompilerParams(vmem_limit_bytes=VMEM_LIMIT),
    )(hid)


def down_kernel(hid_ref, w_ref, out_ref):
    members, height, _ = w_ref.shape
    tiles = hid_ref.shape[1] // LANES
    count = height // tiles
    w = [w_ref[:, q * count : (q + 1) * count].reshape(members * count, LANES) for q in range(tiles)]
    w = jnp.concatenate(w, axis=1)
    out = lax.dot_general(hid_ref[...], w, (((1,), (1,)), ((), ())), preferred_element_type=F32)
    blocks = out_ref.shape[0] // FLIGHT
    for z in range(blocks):
        for x in range(FLIGHT):
            top = (z * FLIGHT + x) * PITCH
            tiles = [out[top : top + PITCH, t : t + LANES] for t in range(0, out.shape[1], LANES)]
            out_ref[x * blocks + z] = jnp.concatenate(tiles, axis=0).astype(BF16)


def down_project(hid, w):
    rows, total = hid.shape
    members, height, _ = w.shape
    cols = members * height * LANES // total
    return pl.pallas_call(
        down_kernel,
        out_shape=jax.ShapeDtypeStruct((rows // PITCH, PITCH * cols // LANES, LANES), BF16),
        compiler_params=pltpu.CompilerParams(vmem_limit_bytes=VMEM_LIMIT),
        cost_estimate=pl.CostEstimate(flops=2 * rows * cols * total, bytes_accessed=2 * total * (cols + rows), transcendentals=0),
    )(hid, w)


def mix_kernel(routes_ref, gates_ref, shrink_ref, home_ref, out_ref):
    taken, first, second = place(routes_ref[...])
    gates = gates_ref[...]
    weight = jnp.where(first, gates[0:1], 0.0) + jnp.where(second, gates[1:2], 0.0)
    weight = jnp.where(taken, weight, 0.0) * shrink_ref[...]
    high = weight.astype(BF16)
    rest = weight - high.astype(F32)
    middle = rest.astype(BF16)
    low = rest - middle.astype(F32)
    weight = jnp.concatenate([low, middle.astype(F32), high.astype(F32)], axis=0).astype(BF16)
    owners, height, _ = home_ref.shape
    blocks = owners // FLIGHT
    tiles = height // PITCH
    cols = tiles * LANES
    piece = cols // blocks
    home = []
    for b in range(blocks):
        each = []
        for e in range(FLIGHT):
            tall = home_ref[e * blocks + b].astype(F32)
            each.append(jnp.concatenate([tall[t * PITCH : (t + 1) * PITCH] for t in range(tiles)], axis=1))
        home.append(jnp.concatenate(each, axis=0) * shrink_ref[...])
    src = lax.broadcasted_iota(jnp.int32, (cols, cols), 0)
    dst = lax.broadcasted_iota(jnp.int32, (cols, cols), 1)
    order = dst == (src & (piece - 1)) * blocks + (src >> (piece.bit_length() - 1))
    order = order.astype(F32).astype(BF16)
    chunks = [jnp.concatenate([h[:, q * piece : (q + 1) * piece] for h in home], axis=1) for q in range(blocks)]
    count = chunks[0].shape[0]
    chunks = jnp.dot(jnp.concatenate(chunks, axis=0).astype(BF16), order, preferred_element_type=F32).astype(BF16)
    for q in range(blocks):
        chunk = chunks[q * count : (q + 1) * count]
        total = lax.dot_general(
            weight, jnp.concatenate([chunk] * 3, axis=0), (((0,), (0,)), ((), ())), preferred_element_type=F32
        )
        out_ref[:, q * cols : (q + 1) * cols] = total.astype(BF16)


def mix(routes_t, gates_t, shrink, home):
    toks = routes_t.shape[1]
    owners, height, _ = home.shape
    width = owners // FLIGHT * height // PITCH * LANES
    return pl.pallas_call(
        mix_kernel,
        out_shape=jax.ShapeDtypeStruct((toks, width), BF16),
        compiler_params=pltpu.CompilerParams(vmem_limit_bytes=VMEM_LIMIT),
    )(routes_t, gates_t, shrink, home)


def on_device(tokens, routes, gate_values, dense_up, dense_down, up_noise):
    flight, _, total = dense_up.shape
    units = up_noise.shape[1]
    blocks = total // units
    here = lax.axis_index("x")
    mine = lax.axis_index("y") * lax.axis_size("core") + lax.axis_index("core")

    got = lax.all_to_all(split(dense_up, dense_down, blocks), ("x", "z"), 0, 0, tiled=True)

    outgoing, shrink = dispatch(routes.T, tokens)
    near = []
    for s in range(flight):
        block = lax.dynamic_index_in_dim(outgoing, (here + s) % flight, 0, keepdims=False)
        near.append(lax.ppermute(block, "x", [(i, (i + s) % flight) for i in range(flight)]) if s else block)
    got, near[1] = lax.optimization_barrier((got, near[1]))
    shard = prepare(mine.reshape(1), got, up_noise.T, total)
    weights = lax.all_gather(shard, ("y", "core"))
    routed = unpack(here.reshape(1), near).astype(jnp.float16)
    routed, _ = lax.optimization_barrier((routed, shard))
    everyone = lax.all_gather(routed, "z", axis=0, tiled=True).astype(BF16)

    hidden, down = up_project(everyone, weights, units)
    hidden = lax.all_gather(hidden.astype(jnp.float16), "z", axis=0, tiled=True).astype(BF16)
    hidden = join(hidden.reshape(blocks, -1, HID_LANES), units)
    out = down_project(hidden, down)
    home = lax.all_to_all(out, ("x", "z"), 0, 0, tiled=True)
    return mix(routes.T, gate_values.T, shrink, home)


def solution(mesh):
    split = Mesh(mesh.devices.reshape(8, 2, 4, 8), ("y", "core", "x", "z"))
    every = ("y", "core", "x", "z")
    return jax.shard_map(
        on_device,
        mesh=split,
        in_specs=(
            P(every, None),
            P(every, None),
            P(every, None),
            P(None, every, None),
            P(None, every, None),
            P(None, ("x", "z")),
        ),
        out_specs=P(every, None),
        check_vma=False,
    )
```

```python
import jax, jax.numpy as jnp
from jax import lax
from jax.experimental import pallas as pl
from jax.experimental.pallas import tpu as pltpu
from jax.sharding import Mesh, PartitionSpec as P

F32, BF16 = jnp.float32, jnp.bfloat16
PITCH, FLIGHT = 12, 4
LANES, HID_LANES, SENT_ROWS = 128, 384, 16
VMEM_LIMIT = 48 * 1024 * 1024
VMEM_SOME = 48_500_000
VMEM_MOST = 62 * 1024 * 1024


def place(routes, here):
    toks = routes.shape[1]
    rows = FLIGHT * PITCH
    slot = lax.broadcasted_iota(jnp.int32, (rows, toks), 0)
    expert = sum((slot >= PITCH * e).astype(jnp.int32) for e in range(1, FLIGHT))
    slot = slot - PITCH * expert
    expert = (expert + here) & (FLIGHT - 1)
    first, second = routes[0:1] == expert, routes[1:2] == expert
    present = jnp.logical_or(first, second)
    earlier = lax.broadcasted_iota(jnp.int32, (toks, toks), 0) < lax.broadcasted_iota(jnp.int32, (toks, toks), 1)
    before = jnp.dot(
        present.astype(F32).astype(BF16), earlier.astype(F32).astype(BF16), preferred_element_type=F32
    )
    taken = jnp.logical_and(present, before == slot.astype(F32))
    return taken, first, second


def rescale(top):
    factor, power = jnp.ones_like(top), jnp.zeros_like(top)
    for bits in (32, 16, 8, 4, 2, 1):
        high = top * (2.0**-bits) >= 8192.0
        scale = jnp.where(high, 2.0**-bits, 1.0)
        top, factor = top * scale, factor * scale
        power = power - jnp.where(high, float(bits), 0.0)
    for bits in (32, 16, 8, 4, 2, 1):
        low = top * (2.0**bits) < 16384.0
        scale = jnp.where(low, 2.0**bits, 1.0)
        top, factor = top * scale, factor * scale
        power = power + jnp.where(low, float(bits), 0.0)
    return factor, power


def dispatch_kernel(here_ref, routes_ref, tokens_ref, *refs):
    out_refs, shrink_ref = refs[:FLIGHT], refs[FLIGHT]
    piece = tokens_ref.shape[1] - out_refs[0].shape[1]
    chunks = tokens_ref.shape[1] // piece
    taken, _, _ = place(routes_ref[...], here_ref[0])
    taken = taken.astype(F32).astype(BF16)
    picked, top = [], None
    for c in range(chunks):
        columns = tokens_ref[:, c * piece : (c + 1) * piece]
        picked.append(jnp.dot(taken, columns, preferred_element_type=F32))
        most = jnp.max(jnp.abs(picked[c]), axis=1, keepdims=True)
        top = most if top is None else jnp.maximum(top, most)
    grow, _ = rescale(top)
    shrink_ref[...] = 1.0 / grow
    rest = picked[-1] * grow
    for c in range(chunks - 1):
        rows = picked[c] * grow
        for e in range(FLIGHT):
            at = e * PITCH
            tails = [rest[at + i : at + i + 1] for i in range(c, PITCH, chunks - 1)]
            out_refs[e][:, c * piece : (c + 1) * piece] = jnp.concatenate([rows[at : at + PITCH]] + tails, axis=0).astype(BF16)


def dispatch(here, routes_t, tokens):
    width = tokens.shape[1]
    chunks = SENT_ROWS // (SENT_ROWS - PITCH)
    piece = width // chunks
    return pl.pallas_call(
        dispatch_kernel,
        in_specs=[
            pl.BlockSpec(memory_space=pltpu.SMEM),
            pl.BlockSpec(memory_space=pltpu.VMEM),
            pl.BlockSpec(memory_space=pltpu.VMEM),
        ],
        out_shape=(
            *[jax.ShapeDtypeStruct((SENT_ROWS, width - piece), BF16)] * FLIGHT,
            jax.ShapeDtypeStruct((FLIGHT * PITCH, 1), F32),
        ),
        compiler_params=pltpu.CompilerParams(vmem_limit_bytes=VMEM_LIMIT),
    )(here, routes_t, tokens)


def unpack_kernel(here_ref, *refs):
    near, rows_ref = refs[:-1], refs[-1]
    here = here_ref[0]
    short = near[0].shape[1]
    rest = rows_ref.shape[1] - short
    fold = short // rest
    blocks = [ref[...].astype(F32) for ref in near]
    rows = []
    for k in range(FLIGHT):
        sent = blocks[(FLIGHT - 1 - k) % FLIGHT]
        for x in range(FLIGHT - 1):
            sent = jnp.where(here == x, blocks[(x - k) % FLIGHT], sent)
        tails = []
        for i in range(PITCH):
            at = PITCH + i // fold
            tails.append(sent[at : at + 1, i % fold * rest : (i % fold + 1) * rest])
        rows.append(jnp.concatenate([sent[:PITCH], jnp.concatenate(tails, axis=0)], axis=1))
    rows_ref[...] = jnp.concatenate(rows, axis=0).astype(BF16)


def unpack(here, near):
    height, short = near[0].shape
    width = short * height // PITCH
    whole = pl.BlockSpec((height, short), lambda i, m: (0, 0))
    return pl.pallas_call(
        unpack_kernel,
        grid_spec=pltpu.PrefetchScalarGridSpec(
            num_scalar_prefetch=1,
            grid=(1,),
            in_specs=[whole] * len(near),
            out_specs=pl.BlockSpec((len(near) * PITCH, width), lambda i, m: (0, 0)),
        ),
        out_shape=jax.ShapeDtypeStruct((len(near) * PITCH, width), BF16),
        compiler_params=pltpu.CompilerParams(vmem_limit_bytes=VMEM_LIMIT),
    )(here, *near)


def split_kernel(up_ref, down_ref, out_ref):
    flight, rows, total = up_ref.shape
    wide = out_ref.shape[2]
    blocks = out_ref.shape[0] // flight
    units = total // blocks
    rim = jnp.zeros((rows, wide - units), F32)
    fill = jnp.zeros((rows - total // wide, wide), F32)
    for e in range(flight):
        up, down = up_ref[e].astype(F32), down_ref[e].astype(F32)
        for b in range(blocks):
            top = jnp.concatenate([up[:, b * units : (b + 1) * units], rim], axis=1)
            row = [down[b : b + 1, at : at + wide] for at in range(0, total, wide)]
            out_ref[e * blocks + b] = jnp.concatenate([top] + row + [fill], axis=0).astype(BF16)


def split(up, down, blocks):
    flight, rows, _ = up.shape
    return pl.pallas_call(
        split_kernel,
        out_shape=jax.ShapeDtypeStruct((flight * blocks, 2 * rows, HID_LANES), BF16),
        compiler_params=pltpu.CompilerParams(vmem_limit_bytes=VMEM_MOST),
    )(up, down)


def prepare_kernel(got_ref, noise_ref, out_ref):
    owners, both, wide = got_ref.shape
    rows = both // 2
    units, span = noise_ref.shape
    got = got_ref[...].astype(F32)
    flat = got[:, :rows, :units].reshape(span, units).astype(BF16)
    same = lax.broadcasted_iota(jnp.int32, (span, span), 0) == lax.broadcasted_iota(jnp.int32, (span, span), 1)
    same = same.astype(F32).astype(BF16)
    up = lax.dot_general(flat, same, (((0,), (0,)), ((), ())), preferred_element_type=F32)
    up = (up + noise_ref[...].astype(F32)).astype(BF16)
    for half in range(span // LANES):
        out_ref[half * units : (half + 1) * units] = up[:, half * LANES : (half + 1) * LANES]
    start = span // LANES * units
    per = wide // LANES
    for q in range((out_ref.shape[0] - start) // owners):
        row = got[:, rows + q // per, q % per * LANES : (q % per + 1) * LANES]
        out_ref[start + q * owners : start + (q + 1) * owners] = row.astype(BF16)


def prepare(got, noise_t, total):
    units, span = noise_t.shape
    height = (span * units + got.shape[0] * total) // LANES
    return pl.pallas_call(
        prepare_kernel,
        out_shape=jax.ShapeDtypeStruct((height, LANES), BF16),
        compiler_params=pltpu.CompilerParams(vmem_limit_bytes=VMEM_LIMIT),
    )(got, noise_t)


def up_kernel(x_ref, w_hbm, out_ref, down_ref, w_ref, sems):
    members, height, _ = w_ref.shape
    chunks = sems.shape[0] - 1
    group = members // chunks
    units = height * LANES * members // x_ref.shape[1]
    parts = height // units
    span = parts * LANES
    copies = []
    for c in range(chunks):
        some = slice(c * group, (c + 1) * group)
        copies.append(pltpu.make_async_copy(w_hbm.at[some, :height], w_ref.at[some], sems.at[c]))
    later = pltpu.make_async_copy(w_hbm.at[:, height:], down_ref, sems.at[chunks])
    for copy in copies + [later]:
        copy.start()
    total = None
    for g in range(members):
        if g % group == 0:
            copies[g // group].wait()
        w = jnp.concatenate([w_ref[g, h * units : (h + 1) * units] for h in range(parts)], axis=1)
        x = x_ref[:, g * span : (g + 1) * span]
        term = lax.dot_general(x, w, (((1,), (1,)), ((), ())), preferred_element_type=F32)
        total = term if total is None else total + term
    hidden = jnp.square(jnp.maximum(total, 0.0))
    factor, power = rescale(jnp.max(hidden, axis=1, keepdims=True))
    hidden = hidden.astype(BF16).astype(F32) * factor
    power = jnp.broadcast_to(power, (power.shape[0], out_ref.shape[1] - units))
    out_ref[...] = jnp.concatenate([hidden, power], axis=1).astype(BF16)
    later.wait()


def up_project(x, w, units, chunks=4):
    rows, width = x.shape
    members, both, _ = w.shape
    height = width // members // LANES * units
    return pl.pallas_call(
        up_kernel,
        in_specs=[pl.BlockSpec(memory_space=pltpu.VMEM), pl.BlockSpec(memory_space=pltpu.HBM)],
        out_specs=(pl.BlockSpec(memory_space=pltpu.VMEM), pl.BlockSpec(memory_space=pltpu.VMEM)),
        out_shape=(
            jax.ShapeDtypeStruct((rows, HID_LANES), BF16),
            jax.ShapeDtypeStruct((members, both - height, LANES), BF16),
        ),
        scratch_shapes=[pltpu.VMEM((members, height, LANES), BF16), pltpu.SemaphoreType.DMA((chunks + 1,))],
        compiler_params=pltpu.CompilerParams(vmem_limit_bytes=VMEM_SOME),
        cost_estimate=pl.CostEstimate(flops=2 * rows * width * units, bytes_accessed=2 * width * (rows + units), transcendentals=0),
    )(x, w)


def join_kernel(units, hid_ref, out_ref):
    hidden = []
    for b in range(hid_ref.shape[0]):
        h = hid_ref[b].astype(F32)
        hidden.append(h[:, :units] * jnp.exp2(-h[:, units : units + 1]))
    out_ref[...] = jnp.concatenate(hidden, axis=1).astype(BF16)


def join(hid, units):
    blocks, rows, _ = hid.shape
    return pl.pallas_call(
        lambda *r: join_kernel(units, *r),
        out_shape=jax.ShapeDtypeStruct((rows, blocks * units), BF16),
        compiler_params=pltpu.CompilerParams(vmem_limit_bytes=VMEM_LIMIT),
    )(hid)


def down_kernel(hid_ref, w_ref, out_ref):
    members, height, _ = w_ref.shape
    tiles = hid_ref.shape[1] // LANES
    count = height // tiles
    w = [w_ref[:, q * count : (q + 1) * count].reshape(members * count, LANES) for q in range(tiles)]
    w = jnp.concatenate(w, axis=1)
    out = lax.dot_general(hid_ref[...], w, (((1,), (1,)), ((), ())), preferred_element_type=F32)
    blocks = out_ref.shape[0] // FLIGHT
    for z in range(blocks):
        for x in range(FLIGHT):
            top = (z * FLIGHT + x) * PITCH
            tiles = [out[top : top + PITCH, t : t + LANES] for t in range(0, out.shape[1], LANES)]
            out_ref[x * blocks + z] = jnp.concatenate(tiles, axis=0).astype(BF16)


def down_project(hid, w):
    rows, total = hid.shape
    members, height, _ = w.shape
    cols = members * height * LANES // total
    return pl.pallas_call(
        down_kernel,
        out_shape=jax.ShapeDtypeStruct((rows // PITCH, PITCH * cols // LANES, LANES), BF16),
        compiler_params=pltpu.CompilerParams(vmem_limit_bytes=VMEM_LIMIT),
        cost_estimate=pl.CostEstimate(flops=2 * rows * cols * total, bytes_accessed=2 * total * (cols + rows), transcendentals=0),
    )(hid, w)


def mix_kernel(here_ref, routes_ref, gates_ref, shrink_ref, home_ref, out_ref):
    taken, first, second = place(routes_ref[...], here_ref[0])
    gates = gates_ref[...]
    weight = jnp.where(first, gates[0:1], 0.0) + jnp.where(second, gates[1:2], 0.0)
    weight = jnp.where(taken, weight, 0.0) * shrink_ref[...]
    high = weight.astype(BF16)
    rest = weight - high.astype(F32)
    middle = rest.astype(BF16)
    low = rest - middle.astype(F32)
    weight = jnp.concatenate([low, middle.astype(F32), high.astype(F32)], axis=0).astype(BF16)
    owners, height, _ = home_ref.shape
    blocks = owners // FLIGHT
    tiles = height // PITCH
    cols = tiles * LANES
    piece = cols // blocks
    home = []
    for b in range(blocks):
        each = []
        for e in range(FLIGHT):
            tall = home_ref[((here_ref[0] + e) & (FLIGHT - 1)) * blocks + b].astype(F32)
            each.append(jnp.concatenate([tall[t * PITCH : (t + 1) * PITCH] for t in range(tiles)], axis=1))
        home.append(jnp.concatenate(each, axis=0) * shrink_ref[...])
    src = lax.broadcasted_iota(jnp.int32, (cols, cols), 0)
    dst = lax.broadcasted_iota(jnp.int32, (cols, cols), 1)
    order = dst == (src & (piece - 1)) * blocks + (src >> (piece.bit_length() - 1))
    order = order.astype(F32).astype(BF16)
    chunks = [jnp.concatenate([h[:, q * piece : (q + 1) * piece] for h in home], axis=1) for q in range(blocks)]
    count = chunks[0].shape[0]
    chunks = jnp.dot(jnp.concatenate(chunks, axis=0).astype(BF16), order, preferred_element_type=F32).astype(BF16)
    for q in range(blocks):
        chunk = chunks[q * count : (q + 1) * count]
        total = lax.dot_general(
            weight, jnp.concatenate([chunk] * 3, axis=0), (((0,), (0,)), ((), ())), preferred_element_type=F32
        )
        out_ref[:, q * cols : (q + 1) * cols] = total.astype(BF16)


def mix(here, routes_t, gates_t, shrink, home):
    toks = routes_t.shape[1]
    owners, height, _ = home.shape
    width = owners // FLIGHT * height // PITCH * LANES
    return pl.pallas_call(
        mix_kernel,
        in_specs=[pl.BlockSpec(memory_space=pltpu.SMEM)] + [pl.BlockSpec(memory_space=pltpu.VMEM)] * 4,
        out_shape=jax.ShapeDtypeStruct((toks, width), BF16),
        compiler_params=pltpu.CompilerParams(vmem_limit_bytes=VMEM_LIMIT),
    )(here, routes_t, gates_t, shrink, home)


def on_device(tokens, routes, gate_values, dense_up, dense_down, up_noise):
    flight, _, total = dense_up.shape
    units = up_noise.shape[1]
    blocks = total // units
    here = lax.axis_index("x").reshape(1)
    mine = lax.axis_index("y") * lax.axis_size("core") + lax.axis_index("core")

    got = lax.all_to_all(split(dense_up, dense_down, blocks), ("x", "z"), 0, 0, tiled=True)

    *near, shrink = dispatch(here, routes.T, tokens)
    for s in range(1, flight):
        near[s] = lax.ppermute(near[s], "x", [(i, (i + s) % flight) for i in range(flight)])
    span = up_noise.shape[0] // lax.axis_size(("y", "core"))
    noise = lax.dynamic_slice_in_dim(up_noise.T, mine * span, span, axis=1)
    got, near[1], noise = lax.optimization_barrier((got, near[1], noise))
    shard = prepare(got, noise, total)
    weights = lax.all_gather(shard, ("y", "core"))
    routed = unpack(here, near).astype(jnp.float16)
    routed, _ = lax.optimization_barrier((routed, shard))
    everyone = lax.all_gather(routed, "z", axis=0, tiled=True).astype(BF16)

    hidden, down = up_project(everyone, weights, units)
    hidden = lax.all_gather(hidden.astype(jnp.float16), "z", axis=0, tiled=True).astype(BF16)
    hidden = join(hidden.reshape(blocks, -1, HID_LANES), units)
    out = down_project(hidden, down)
    home = lax.all_to_all(out, ("x", "z"), 0, 0, tiled=True)
    return mix(here, routes.T, gate_values.T, shrink, home)


def solution(mesh):
    split = Mesh(mesh.devices.reshape(8, 2, 4, 8), ("y", "core", "x", "z"))
    every = ("y", "core", "x", "z")
    return jax.shard_map(
        on_device,
        mesh=split,
        in_specs=(
            P(every, None),
            P(every, None),
            P(every, None),
            P(None, every, None),
            P(None, every, None),
            P(None, ("x", "z")),
        ),
        out_specs=P(every, None),
        check_vma=False,
    )
```

```python
import jax, jax.numpy as jnp
from jax import lax
from jax.experimental import pallas as pl
from jax.experimental.pallas import tpu as pltpu
from jax.sharding import Mesh, PartitionSpec as P

F32, BF16 = jnp.float32, jnp.bfloat16
PITCH, FLIGHT = 12, 4
LANES, HID_LANES, SENT_ROWS = 128, 384, 16
VMEM_LIMIT = 48 * 1024 * 1024
VMEM_SOME = 48_500_000
VMEM_MOST = 62 * 1024 * 1024


def place(routes, here):
    toks = routes.shape[1]
    rows = FLIGHT * PITCH
    slot = lax.broadcasted_iota(jnp.int32, (rows, toks), 0)
    expert = sum((slot >= PITCH * e).astype(jnp.int32) for e in range(1, FLIGHT))
    slot = slot - PITCH * expert
    expert = (expert + here) & (FLIGHT - 1)
    first, second = routes[0:1] == expert, routes[1:2] == expert
    present = jnp.logical_or(first, second)
    earlier = lax.broadcasted_iota(jnp.int32, (toks, toks), 0) < lax.broadcasted_iota(jnp.int32, (toks, toks), 1)
    before = jnp.dot(
        present.astype(F32).astype(BF16), earlier.astype(F32).astype(BF16), preferred_element_type=F32
    )
    taken = jnp.logical_and(present, before == slot.astype(F32))
    return taken, first, second


def rescale(top):
    factor, power = jnp.ones_like(top), jnp.zeros_like(top)
    for bits in (32, 16, 8, 4, 2, 1):
        high = top * (2.0**-bits) >= 8192.0
        scale = jnp.where(high, 2.0**-bits, 1.0)
        top, factor = top * scale, factor * scale
        power = power - jnp.where(high, float(bits), 0.0)
    for bits in (32, 16, 8, 4, 2, 1):
        low = top * (2.0**bits) < 16384.0
        scale = jnp.where(low, 2.0**bits, 1.0)
        top, factor = top * scale, factor * scale
        power = power + jnp.where(low, float(bits), 0.0)
    return factor, power


def dispatch_kernel(here_ref, routes_ref, tokens_ref, *refs):
    out_refs, shrink_ref = refs[:FLIGHT], refs[FLIGHT]
    piece = tokens_ref.shape[1] - out_refs[0].shape[1]
    chunks = tokens_ref.shape[1] // piece
    taken, _, _ = place(routes_ref[...], here_ref[0])
    taken = taken.astype(F32).astype(BF16)
    picked, top = [], None
    for c in range(chunks):
        columns = tokens_ref[:, c * piece : (c + 1) * piece]
        picked.append(jnp.dot(taken, columns, preferred_element_type=F32))
        most = jnp.max(jnp.abs(picked[c]), axis=1, keepdims=True)
        top = most if top is None else jnp.maximum(top, most)
    grow, _ = rescale(top)
    shrink_ref[...] = 1.0 / grow
    rest = picked[-1] * grow
    for c in range(chunks - 1):
        rows = picked[c] * grow
        for e in range(FLIGHT):
            at = e * PITCH
            tails = [rest[at + i : at + i + 1] for i in range(c, PITCH, chunks - 1)]
            out_refs[e][:, c * piece : (c + 1) * piece] = jnp.concatenate([rows[at : at + PITCH]] + tails, axis=0).astype(BF16)


def dispatch(here, routes_t, tokens):
    width = tokens.shape[1]
    chunks = SENT_ROWS // (SENT_ROWS - PITCH)
    piece = width // chunks
    return pl.pallas_call(
        dispatch_kernel,
        in_specs=[
            pl.BlockSpec(memory_space=pltpu.SMEM),
            pl.BlockSpec(memory_space=pltpu.VMEM),
            pl.BlockSpec(memory_space=pltpu.VMEM),
        ],
        out_shape=(
            *[jax.ShapeDtypeStruct((SENT_ROWS, width - piece), BF16)] * FLIGHT,
            jax.ShapeDtypeStruct((FLIGHT * PITCH, 1), F32),
        ),
        compiler_params=pltpu.CompilerParams(vmem_limit_bytes=VMEM_LIMIT),
    )(here, routes_t, tokens)


def unpack_kernel(here_ref, *refs):
    near, rows_ref = refs[:-1], refs[-1]
    here = here_ref[0]
    short = near[0].shape[1]
    rest = rows_ref.shape[1] - short
    fold = short // rest
    blocks = [ref[...].astype(F32) for ref in near]
    rows = []
    for k in range(FLIGHT):
        sent = blocks[(FLIGHT - 1 - k) % FLIGHT]
        for x in range(FLIGHT - 1):
            sent = jnp.where(here == x, blocks[(x - k) % FLIGHT], sent)
        tails = []
        for i in range(PITCH):
            at = PITCH + i // fold
            tails.append(sent[at : at + 1, i % fold * rest : (i % fold + 1) * rest])
        rows.append(jnp.concatenate([sent[:PITCH], jnp.concatenate(tails, axis=0)], axis=1))
    rows_ref[...] = jnp.concatenate(rows, axis=0).astype(BF16)


def unpack(here, near):
    height, short = near[0].shape
    width = short * height // PITCH
    whole = pl.BlockSpec((height, short), lambda i, m: (0, 0))
    return pl.pallas_call(
        unpack_kernel,
        grid_spec=pltpu.PrefetchScalarGridSpec(
            num_scalar_prefetch=1,
            grid=(1,),
            in_specs=[whole] * len(near),
            out_specs=pl.BlockSpec((len(near) * PITCH, width), lambda i, m: (0, 0)),
        ),
        out_shape=jax.ShapeDtypeStruct((len(near) * PITCH, width), BF16),
        compiler_params=pltpu.CompilerParams(vmem_limit_bytes=VMEM_LIMIT),
    )(here, *near)


def split_kernel(up_ref, down_ref, out_ref):
    flight, rows, total = up_ref.shape
    wide = out_ref.shape[2]
    blocks = out_ref.shape[0] // flight
    units = total // blocks
    rim = jnp.zeros((rows, wide - units), F32)
    fill = jnp.zeros((rows - total // wide, wide), F32)
    for e in range(flight):
        up, down = up_ref[e].astype(F32), down_ref[e].astype(F32)
        for b in range(blocks):
            top = jnp.concatenate([up[:, b * units : (b + 1) * units], rim], axis=1)
            row = [down[b : b + 1, at : at + wide] for at in range(0, total, wide)]
            out_ref[e * blocks + b] = jnp.concatenate([top] + row + [fill], axis=0).astype(BF16)


def split(up, down, blocks):
    flight, rows, _ = up.shape
    return pl.pallas_call(
        split_kernel,
        out_shape=jax.ShapeDtypeStruct((flight * blocks, 2 * rows, HID_LANES), BF16),
        compiler_params=pltpu.CompilerParams(vmem_limit_bytes=VMEM_MOST),
    )(up, down)


def prepare_kernel(got_ref, noise_ref, out_ref):
    owners, both, wide = got_ref.shape
    rows = both // 2
    units, span = noise_ref.shape
    got = got_ref[...].astype(F32)
    flat = got[:, :rows, :units].reshape(span, units).astype(BF16)
    same = lax.broadcasted_iota(jnp.int32, (span, span), 0) == lax.broadcasted_iota(jnp.int32, (span, span), 1)
    same = same.astype(F32).astype(BF16)
    up = lax.dot_general(flat, same, (((0,), (0,)), ((), ())), preferred_element_type=F32)
    up = (up + noise_ref[...].astype(F32)).astype(BF16)
    for half in range(span // LANES):
        out_ref[half * units : (half + 1) * units] = up[:, half * LANES : (half + 1) * LANES]
    start = span // LANES * units
    per = wide // LANES
    for q in range((out_ref.shape[0] - start) // owners):
        row = got[:, rows + q // per, q % per * LANES : (q % per + 1) * LANES]
        out_ref[start + q * owners : start + (q + 1) * owners] = row.astype(BF16)


def prepare(got, noise_t, total):
    units, span = noise_t.shape
    height = (span * units + got.shape[0] * total) // LANES
    return pl.pallas_call(
        prepare_kernel,
        out_shape=jax.ShapeDtypeStruct((height, LANES), BF16),
        compiler_params=pltpu.CompilerParams(vmem_limit_bytes=VMEM_LIMIT),
    )(got, noise_t)


def up_kernel(x_ref, w_hbm, out_ref, down_ref, w_ref, sems):
    members, height, _ = w_ref.shape
    chunks = sems.shape[0] - 1
    group = members // chunks
    units = height * LANES * members // x_ref.shape[1]
    parts = height // units
    span = parts * LANES
    copies = []
    for c in range(chunks):
        some = slice(c * group, (c + 1) * group)
        copies.append(pltpu.make_async_copy(w_hbm.at[some, :height], w_ref.at[some], sems.at[c]))
    later = pltpu.make_async_copy(w_hbm.at[:, height:], down_ref, sems.at[chunks])
    for copy in copies + [later]:
        copy.start()
    total = None
    for g in range(members):
        if g % group == 0:
            copies[g // group].wait()
        w = jnp.concatenate([w_ref[g, h * units : (h + 1) * units] for h in range(parts)], axis=1)
        x = x_ref[:, g * span : (g + 1) * span]
        term = lax.dot_general(x, w, (((1,), (1,)), ((), ())), preferred_element_type=F32)
        total = term if total is None else total + term
    hidden = jnp.square(jnp.maximum(total, 0.0))
    factor, power = rescale(jnp.max(hidden, axis=1, keepdims=True))
    hidden = hidden.astype(BF16).astype(F32) * factor
    power = jnp.broadcast_to(power, (power.shape[0], out_ref.shape[1] - units))
    out_ref[...] = jnp.concatenate([hidden, power], axis=1).astype(BF16)
    later.wait()


def up_project(x, w, units, chunks=4):
    rows, width = x.shape
    members, both, _ = w.shape
    height = width // members // LANES * units
    return pl.pallas_call(
        up_kernel,
        in_specs=[pl.BlockSpec(memory_space=pltpu.VMEM), pl.BlockSpec(memory_space=pltpu.HBM)],
        out_specs=(pl.BlockSpec(memory_space=pltpu.VMEM), pl.BlockSpec(memory_space=pltpu.VMEM)),
        out_shape=(
            jax.ShapeDtypeStruct((rows, HID_LANES), BF16),
            jax.ShapeDtypeStruct((members, both - height, LANES), BF16),
        ),
        scratch_shapes=[pltpu.VMEM((members, height, LANES), BF16), pltpu.SemaphoreType.DMA((chunks + 1,))],
        compiler_params=pltpu.CompilerParams(vmem_limit_bytes=VMEM_SOME),
        cost_estimate=pl.CostEstimate(flops=2 * rows * width * units, bytes_accessed=2 * width * (rows + units), transcendentals=0),
    )(x, w)


def join_kernel(units, hid_ref, out_ref):
    hidden = []
    for b in range(hid_ref.shape[0]):
        h = hid_ref[b].astype(F32)
        hidden.append(h[:, :units] * jnp.exp2(-h[:, units : units + 1]))
    out_ref[...] = jnp.concatenate(hidden, axis=1).astype(BF16)


def join(hid, units):
    blocks, rows, _ = hid.shape
    return pl.pallas_call(
        lambda *r: join_kernel(units, *r),
        out_shape=jax.ShapeDtypeStruct((rows, blocks * units), BF16),
        compiler_params=pltpu.CompilerParams(vmem_limit_bytes=VMEM_LIMIT),
    )(hid)


def down_kernel(hid_ref, w_ref, out_ref):
    members, height, _ = w_ref.shape
    tiles = hid_ref.shape[1] // LANES
    count = height // tiles
    w = [w_ref[:, q * count : (q + 1) * count].reshape(members * count, LANES) for q in range(tiles)]
    w = jnp.concatenate(w, axis=1)
    out = lax.dot_general(hid_ref[...], w, (((1,), (1,)), ((), ())), preferred_element_type=F32)
    blocks = out_ref.shape[0] // FLIGHT
    for z in range(blocks):
        for x in range(FLIGHT):
            top = (z * FLIGHT + x) * PITCH
            tiles = [out[top : top + PITCH, t : t + LANES] for t in range(0, out.shape[1], LANES)]
            out_ref[x * blocks + z] = jnp.concatenate(tiles, axis=0).astype(BF16)


def down_project(hid, w):
    rows, total = hid.shape
    members, height, _ = w.shape
    cols = members * height * LANES // total
    return pl.pallas_call(
        down_kernel,
        out_shape=jax.ShapeDtypeStruct((rows // PITCH, PITCH * cols // LANES, LANES), BF16),
        compiler_params=pltpu.CompilerParams(vmem_limit_bytes=VMEM_LIMIT),
        cost_estimate=pl.CostEstimate(flops=2 * rows * cols * total, bytes_accessed=2 * total * (cols + rows), transcendentals=0),
    )(hid, w)


def mix_kernel(here_ref, routes_ref, gates_ref, shrink_ref, home_ref, out_ref):
    taken, first, second = place(routes_ref[...], here_ref[0])
    gates = gates_ref[...]
    weight = jnp.where(first, gates[0:1], 0.0) + jnp.where(second, gates[1:2], 0.0)
    weight = jnp.where(taken, weight, 0.0) * shrink_ref[...]
    high = weight.astype(BF16)
    rest = weight - high.astype(F32)
    middle = rest.astype(BF16)
    low = rest - middle.astype(F32)
    weight = jnp.concatenate([low, middle.astype(F32), high.astype(F32)], axis=0).astype(BF16)
    owners, height, _ = home_ref.shape
    blocks = owners // FLIGHT
    tiles = height // PITCH
    cols = tiles * LANES
    piece = cols // blocks
    home = []
    for b in range(blocks):
        each = []
        for e in range(FLIGHT):
            tall = home_ref[((here_ref[0] + e) & (FLIGHT - 1)) * blocks + b].astype(F32)
            each.append(jnp.concatenate([tall[t * PITCH : (t + 1) * PITCH] for t in range(tiles)], axis=1))
        home.append(jnp.concatenate(each, axis=0) * shrink_ref[...])
    src = lax.broadcasted_iota(jnp.int32, (cols, cols), 0)
    dst = lax.broadcasted_iota(jnp.int32, (cols, cols), 1)
    order = dst == (src & (piece - 1)) * blocks + (src >> (piece.bit_length() - 1))
    order = order.astype(F32).astype(BF16)
    chunks = [jnp.concatenate([h[:, q * piece : (q + 1) * piece] for h in home], axis=1) for q in range(blocks)]
    count = chunks[0].shape[0]
    chunks = jnp.dot(jnp.concatenate(chunks, axis=0).astype(BF16), order, preferred_element_type=F32).astype(BF16)
    for q in range(blocks):
        chunk = chunks[q * count : (q + 1) * count]
        total = lax.dot_general(
            weight, jnp.concatenate([chunk] * 3, axis=0), (((0,), (0,)), ((), ())), preferred_element_type=F32
        )
        out_ref[:, q * cols : (q + 1) * cols] = total.astype(BF16)


def mix(here, routes_t, gates_t, shrink, home):
    toks = routes_t.shape[1]
    owners, height, _ = home.shape
    width = owners // FLIGHT * height // PITCH * LANES
    return pl.pallas_call(
        mix_kernel,
        in_specs=[pl.BlockSpec(memory_space=pltpu.SMEM)] + [pl.BlockSpec(memory_space=pltpu.VMEM)] * 4,
        out_shape=jax.ShapeDtypeStruct((toks, width), BF16),
        compiler_params=pltpu.CompilerParams(vmem_limit_bytes=VMEM_LIMIT),
    )(here, routes_t, gates_t, shrink, home)


def on_device(tokens, routes, gate_values, dense_up, dense_down, up_noise):
    flight, _, total = dense_up.shape
    units = up_noise.shape[1]
    blocks = total // units
    here = lax.axis_index("x").reshape(1)
    mine = lax.axis_index("y") * lax.axis_size("core") + lax.axis_index("core")

    got = lax.all_to_all(split(dense_up, dense_down, blocks), ("x", "z"), 0, 0, tiled=True)

    *near, shrink = dispatch(here, routes.T, tokens)
    for s in range(1, flight):
        near[s] = lax.ppermute(near[s], "x", [(i, (i + s) % flight) for i in range(flight)])
    span = up_noise.shape[0] // lax.axis_size(("y", "core"))
    noise = lax.dynamic_slice_in_dim(up_noise.T, mine * span, span, axis=1)
    got, near[1], near[2], noise = lax.optimization_barrier((got, near[1], near[2], noise))
    shard = prepare(got, noise, total)
    weights = lax.all_gather(shard, ("y", "core"))
    routed = unpack(here, near).astype(jnp.float16)
    routed, _ = lax.optimization_barrier((routed, shard))
    everyone = lax.all_gather(routed, "z", axis=0, tiled=True).astype(BF16)

    hidden, down = up_project(everyone, weights, units)
    hidden = lax.all_gather(hidden.astype(jnp.float16), "z", axis=0, tiled=True).astype(BF16)
    hidden = join(hidden.reshape(blocks, -1, HID_LANES), units)
    out = down_project(hidden, down)
    home = lax.all_to_all(out, ("x", "z"), 0, 0, tiled=True)
    return mix(here, routes.T, gate_values.T, shrink, home)


def solution(mesh):
    split = Mesh(mesh.devices.reshape(8, 2, 4, 8), ("y", "core", "x", "z"))
    every = ("y", "core", "x", "z")
    return jax.shard_map(
        on_device,
        mesh=split,
        in_specs=(
            P(every, None),
            P(every, None),
            P(every, None),
            P(None, every, None),
            P(None, every, None),
            P(None, ("x", "z")),
        ),
        out_specs=P(every, None),
        check_vma=False,
    )
```

```python
import jax, jax.numpy as jnp
from jax import lax
from jax.experimental import pallas as pl
from jax.experimental.pallas import tpu as pltpu
from jax.sharding import Mesh, PartitionSpec as P

F32, BF16 = jnp.float32, jnp.bfloat16
PITCH, FLIGHT = 12, 4
LANES, HID_LANES, SENT_ROWS = 128, 384, 16
VMEM_LIMIT = 48 * 1024 * 1024
VMEM_SOME = 48_500_000
VMEM_MOST = 62 * 1024 * 1024


def place(routes, here):
    toks = routes.shape[1]
    rows = FLIGHT * PITCH
    slot = lax.broadcasted_iota(jnp.int32, (rows, toks), 0)
    expert = sum((slot >= PITCH * e).astype(jnp.int32) for e in range(1, FLIGHT))
    slot = slot - PITCH * expert
    expert = (expert + here) & (FLIGHT - 1)
    first, second = routes[0:1] == expert, routes[1:2] == expert
    present = jnp.logical_or(first, second)
    earlier = lax.broadcasted_iota(jnp.int32, (toks, toks), 0) < lax.broadcasted_iota(jnp.int32, (toks, toks), 1)
    before = jnp.dot(
        present.astype(F32).astype(BF16), earlier.astype(F32).astype(BF16), preferred_element_type=F32
    )
    taken = jnp.logical_and(present, before == slot.astype(F32))
    return taken, first, second


def rescale(top):
    factor, power = jnp.ones_like(top), jnp.zeros_like(top)
    for bits in (32, 16, 8, 4, 2, 1):
        high = top * (2.0**-bits) >= 8192.0
        scale = jnp.where(high, 2.0**-bits, 1.0)
        top, factor = top * scale, factor * scale
        power = power - jnp.where(high, float(bits), 0.0)
    for bits in (32, 16, 8, 4, 2, 1):
        low = top * (2.0**bits) < 16384.0
        scale = jnp.where(low, 2.0**bits, 1.0)
        top, factor = top * scale, factor * scale
        power = power + jnp.where(low, float(bits), 0.0)
    return factor, power


def dispatch_kernel(here_ref, routes_ref, tokens_ref, out_ref, shrink_ref):
    piece = tokens_ref.shape[1] - out_ref.shape[2]
    chunks = tokens_ref.shape[1] // piece
    taken, _, _ = place(routes_ref[...], here_ref[0])
    taken = taken.astype(F32).astype(BF16)
    picked, top = [], None
    for c in range(chunks):
        columns = tokens_ref[:, c * piece : (c + 1) * piece]
        picked.append(jnp.dot(taken, columns, preferred_element_type=F32))
        most = jnp.max(jnp.abs(picked[c]), axis=1, keepdims=True)
        top = most if top is None else jnp.maximum(top, most)
    grow, _ = rescale(top)
    shrink_ref[...] = 1.0 / grow
    rest = picked[-1] * grow
    for c in range(chunks - 1):
        rows = picked[c] * grow
        for e in range(FLIGHT):
            at = e * PITCH
            tails = [rest[at + i : at + i + 1] for i in range(c, PITCH, chunks - 1)]
            out_ref[e, :, c * piece : (c + 1) * piece] = jnp.concatenate([rows[at : at + PITCH]] + tails, axis=0).astype(BF16)


def dispatch(here, routes_t, tokens):
    width = tokens.shape[1]
    chunks = SENT_ROWS // (SENT_ROWS - PITCH)
    piece = width // chunks
    return pl.pallas_call(
        dispatch_kernel,
        in_specs=[
            pl.BlockSpec(memory_space=pltpu.SMEM),
            pl.BlockSpec(memory_space=pltpu.VMEM),
            pl.BlockSpec(memory_space=pltpu.VMEM),
        ],
        out_shape=(
            jax.ShapeDtypeStruct((FLIGHT, SENT_ROWS, width - piece), BF16),
            jax.ShapeDtypeStruct((FLIGHT * PITCH, 1), F32),
        ),
        compiler_params=pltpu.CompilerParams(vmem_limit_bytes=VMEM_LIMIT),
    )(here, routes_t, tokens)


def unpack_kernel(near_ref, rows_ref):
    short = near_ref.shape[2]
    rest = rows_ref.shape[1] - short
    fold = short // rest
    rows = []
    for e in range(FLIGHT):
        sent = near_ref[e].astype(F32)
        tails = []
        for i in range(PITCH):
            at = PITCH + i // fold
            tails.append(sent[at : at + 1, i % fold * rest : (i % fold + 1) * rest])
        rows.append(jnp.concatenate([sent[:PITCH], jnp.concatenate(tails, axis=0)], axis=1))
    rows_ref[...] = jnp.concatenate(rows, axis=0).astype(BF16)


def unpack(near):
    flight, height, short = near.shape
    return pl.pallas_call(
        unpack_kernel,
        out_shape=jax.ShapeDtypeStruct((flight * PITCH, short * height // PITCH), BF16),
        compiler_params=pltpu.CompilerParams(vmem_limit_bytes=VMEM_LIMIT),
    )(near)


def split_kernel(up_ref, down_ref, out_ref):
    flight, rows, total = up_ref.shape
    wide = out_ref.shape[2]
    blocks = out_ref.shape[0] // flight
    units = total // blocks
    rim = jnp.zeros((rows, wide - units), F32)
    fill = jnp.zeros((rows - total // wide, wide), F32)
    for e in range(flight):
        up, down = up_ref[e].astype(F32), down_ref[e].astype(F32)
        for b in range(blocks):
            top = jnp.concatenate([up[:, b * units : (b + 1) * units], rim], axis=1)
            row = [down[b : b + 1, at : at + wide] for at in range(0, total, wide)]
            out_ref[e * blocks + b] = jnp.concatenate([top] + row + [fill], axis=0).astype(BF16)


def split(up, down, blocks):
    flight, rows, _ = up.shape
    return pl.pallas_call(
        split_kernel,
        out_shape=jax.ShapeDtypeStruct((flight * blocks, 2 * rows, HID_LANES), BF16),
        compiler_params=pltpu.CompilerParams(vmem_limit_bytes=VMEM_MOST),
    )(up, down)


def prepare_kernel(got_ref, noise_ref, out_ref):
    owners, both, wide = got_ref.shape
    rows = both // 2
    units, span = noise_ref.shape
    got = got_ref[...].astype(F32)
    flat = got[:, :rows, :units].reshape(span, units).astype(BF16)
    same = lax.broadcasted_iota(jnp.int32, (span, span), 0) == lax.broadcasted_iota(jnp.int32, (span, span), 1)
    same = same.astype(F32).astype(BF16)
    up = lax.dot_general(flat, same, (((0,), (0,)), ((), ())), preferred_element_type=F32)
    up = (up + noise_ref[...].astype(F32)).astype(BF16)
    for half in range(span // LANES):
        out_ref[half * units : (half + 1) * units] = up[:, half * LANES : (half + 1) * LANES]
    start = span // LANES * units
    per = wide // LANES
    for q in range((out_ref.shape[0] - start) // owners):
        row = got[:, rows + q // per, q % per * LANES : (q % per + 1) * LANES]
        out_ref[start + q * owners : start + (q + 1) * owners] = row.astype(BF16)


def prepare(got, noise_t, total):
    units, span = noise_t.shape
    height = (span * units + got.shape[0] * total) // LANES
    return pl.pallas_call(
        prepare_kernel,
        out_shape=jax.ShapeDtypeStruct((height, LANES), BF16),
        compiler_params=pltpu.CompilerParams(vmem_limit_bytes=VMEM_LIMIT),
    )(got, noise_t)


def up_kernel(x_ref, w_hbm, out_ref, down_ref, w_ref, sems):
    members, height, _ = w_ref.shape
    chunks = sems.shape[0] - 1
    group = members // chunks
    units = height * LANES * members // x_ref.shape[1]
    parts = height // units
    span = parts * LANES
    copies = []
    for c in range(chunks):
        some = slice(c * group, (c + 1) * group)
        copies.append(pltpu.make_async_copy(w_hbm.at[some, :height], w_ref.at[some], sems.at[c]))
    later = pltpu.make_async_copy(w_hbm.at[:, height:], down_ref, sems.at[chunks])
    for copy in copies + [later]:
        copy.start()
    total = None
    for g in range(members):
        if g % group == 0:
            copies[g // group].wait()
        w = jnp.concatenate([w_ref[g, h * units : (h + 1) * units] for h in range(parts)], axis=1)
        x = x_ref[:, g * span : (g + 1) * span]
        term = lax.dot_general(x, w, (((1,), (1,)), ((), ())), preferred_element_type=F32)
        total = term if total is None else total + term
    hidden = jnp.square(jnp.maximum(total, 0.0))
    factor, power = rescale(jnp.max(hidden, axis=1, keepdims=True))
    hidden = hidden.astype(BF16).astype(F32) * factor
    power = jnp.broadcast_to(power, (power.shape[0], out_ref.shape[1] - units))
    out_ref[...] = jnp.concatenate([hidden, power], axis=1).astype(BF16)
    later.wait()


def up_project(x, w, units, chunks=4):
    rows, width = x.shape
    members, both, _ = w.shape
    height = width // members // LANES * units
    return pl.pallas_call(
        up_kernel,
        in_specs=[pl.BlockSpec(memory_space=pltpu.VMEM), pl.BlockSpec(memory_space=pltpu.HBM)],
        out_specs=(pl.BlockSpec(memory_space=pltpu.VMEM), pl.BlockSpec(memory_space=pltpu.VMEM)),
        out_shape=(
            jax.ShapeDtypeStruct((rows, HID_LANES), BF16),
            jax.ShapeDtypeStruct((members, both - height, LANES), BF16),
        ),
        scratch_shapes=[pltpu.VMEM((members, height, LANES), BF16), pltpu.SemaphoreType.DMA((chunks + 1,))],
        compiler_params=pltpu.CompilerParams(vmem_limit_bytes=VMEM_SOME),
        cost_estimate=pl.CostEstimate(flops=2 * rows * width * units, bytes_accessed=2 * width * (rows + units), transcendentals=0),
    )(x, w)


def join_kernel(units, hid_ref, out_ref):
    hidden = []
    for b in range(hid_ref.shape[0]):
        h = hid_ref[b].astype(F32)
        hidden.append(h[:, :units] * jnp.exp2(-h[:, units : units + 1]))
    out_ref[...] = jnp.concatenate(hidden, axis=1).astype(BF16)


def join(hid, units):
    blocks, rows, _ = hid.shape
    return pl.pallas_call(
        lambda *r: join_kernel(units, *r),
        out_shape=jax.ShapeDtypeStruct((rows, blocks * units), BF16),
        compiler_params=pltpu.CompilerParams(vmem_limit_bytes=VMEM_LIMIT),
    )(hid)


def down_kernel(hid_ref, w_ref, out_ref):
    members, height, _ = w_ref.shape
    tiles = hid_ref.shape[1] // LANES
    count = height // tiles
    w = [w_ref[:, q * count : (q + 1) * count].reshape(members * count, LANES) for q in range(tiles)]
    w = jnp.concatenate(w, axis=1)
    out = lax.dot_general(hid_ref[...], w, (((1,), (1,)), ((), ())), preferred_element_type=F32)
    blocks = out_ref.shape[0] // FLIGHT
    for z in range(blocks):
        for x in range(FLIGHT):
            top = (z * FLIGHT + x) * PITCH
            tiles = [out[top : top + PITCH, t : t + LANES] for t in range(0, out.shape[1], LANES)]
            out_ref[x * blocks + z] = jnp.concatenate(tiles, axis=0).astype(BF16)


def down_project(hid, w):
    rows, total = hid.shape
    members, height, _ = w.shape
    cols = members * height * LANES // total
    return pl.pallas_call(
        down_kernel,
        out_shape=jax.ShapeDtypeStruct((rows // PITCH, PITCH * cols // LANES, LANES), BF16),
        compiler_params=pltpu.CompilerParams(vmem_limit_bytes=VMEM_LIMIT),
        cost_estimate=pl.CostEstimate(flops=2 * rows * cols * total, bytes_accessed=2 * total * (cols + rows), transcendentals=0),
    )(hid, w)


def mix_kernel(here_ref, routes_ref, gates_ref, shrink_ref, home_ref, out_ref):
    taken, first, second = place(routes_ref[...], here_ref[0])
    gates = gates_ref[...]
    weight = jnp.where(first, gates[0:1], 0.0) + jnp.where(second, gates[1:2], 0.0)
    weight = jnp.where(taken, weight, 0.0) * shrink_ref[...]
    high = weight.astype(BF16)
    rest = weight - high.astype(F32)
    middle = rest.astype(BF16)
    low = rest - middle.astype(F32)
    weight = jnp.concatenate([low, middle.astype(F32), high.astype(F32)], axis=0).astype(BF16)
    owners, height, _ = home_ref.shape
    blocks = owners // FLIGHT
    tiles = height // PITCH
    cols = tiles * LANES
    piece = cols // blocks
    home = []
    for b in range(blocks):
        each = []
        for e in range(FLIGHT):
            tall = home_ref[((here_ref[0] + e) & (FLIGHT - 1)) * blocks + b].astype(F32)
            each.append(jnp.concatenate([tall[t * PITCH : (t + 1) * PITCH] for t in range(tiles)], axis=1))
        home.append(jnp.concatenate(each, axis=0) * shrink_ref[...])
    src = lax.broadcasted_iota(jnp.int32, (cols, cols), 0)
    dst = lax.broadcasted_iota(jnp.int32, (cols, cols), 1)
    order = dst == (src & (piece - 1)) * blocks + (src >> (piece.bit_length() - 1))
    order = order.astype(F32).astype(BF16)
    chunks = [jnp.concatenate([h[:, q * piece : (q + 1) * piece] for h in home], axis=1) for q in range(blocks)]
    count = chunks[0].shape[0]
    chunks = jnp.dot(jnp.concatenate(chunks, axis=0).astype(BF16), order, preferred_element_type=F32).astype(BF16)
    for q in range(blocks):
        chunk = chunks[q * count : (q + 1) * count]
        total = lax.dot_general(
            weight, jnp.concatenate([chunk] * 3, axis=0), (((0,), (0,)), ((), ())), preferred_element_type=F32
        )
        out_ref[:, q * cols : (q + 1) * cols] = total.astype(BF16)


def mix(here, routes_t, gates_t, shrink, home):
    toks = routes_t.shape[1]
    owners, height, _ = home.shape
    width = owners // FLIGHT * height // PITCH * LANES
    return pl.pallas_call(
        mix_kernel,
        in_specs=[pl.BlockSpec(memory_space=pltpu.SMEM)] + [pl.BlockSpec(memory_space=pltpu.VMEM)] * 4,
        out_shape=jax.ShapeDtypeStruct((toks, width), BF16),
        compiler_params=pltpu.CompilerParams(vmem_limit_bytes=VMEM_LIMIT),
    )(here, routes_t, gates_t, shrink, home)


def on_device(tokens, routes, gate_values, dense_up, dense_down, up_noise):
    flight, _, total = dense_up.shape
    units = up_noise.shape[1]
    blocks = total // units
    here = jnp.zeros((1,), jnp.int32)
    mine = lax.axis_index("y") * lax.axis_size("core") + lax.axis_index("core")

    got = lax.all_to_all(split(dense_up, dense_down, blocks), ("x", "z"), 0, 0, tiled=True)

    outgoing, shrink = dispatch(here, routes.T, tokens)
    span = up_noise.shape[0] // lax.axis_size(("y", "core"))
    noise = lax.dynamic_slice_in_dim(up_noise.T, mine * span, span, axis=1)
    got, outgoing, noise = lax.optimization_barrier((got, outgoing, noise))
    shard = prepare(got, noise, total)
    weights = lax.all_gather(shard, ("y", "core"))
    outgoing, _ = lax.optimization_barrier((outgoing, shard))
    near = lax.all_to_all(outgoing, "x", 0, 0, tiled=True)
    routed = unpack(near).astype(jnp.float16)
    routed, _ = lax.optimization_barrier((routed, shard))
    everyone = lax.all_gather(routed, "z", axis=0, tiled=True).astype(BF16)

    hidden, down = up_project(everyone, weights, units)
    hidden = lax.all_gather(hidden.astype(jnp.float16), "z", axis=0, tiled=True).astype(BF16)
    hidden = join(hidden.reshape(blocks, -1, HID_LANES), units)
    out = down_project(hidden, down)
    home = lax.all_to_all(out, ("x", "z"), 0, 0, tiled=True)
    return mix(here, routes.T, gate_values.T, shrink, home)


def solution(mesh):
    split = Mesh(mesh.devices.reshape(8, 2, 4, 8), ("y", "core", "x", "z"))
    every = ("y", "core", "x", "z")
    return jax.shard_map(
        on_device,
        mesh=split,
        in_specs=(
            P(every, None),
            P(every, None),
            P(every, None),
            P(None, every, None),
            P(None, every, None),
            P(None, ("x", "z")),
        ),
        out_specs=P(every, None),
        check_vma=False,
    )
```

```python
import jax, jax.numpy as jnp
from jax import lax
from jax.experimental import pallas as pl
from jax.experimental.pallas import tpu as pltpu
from jax.sharding import Mesh, PartitionSpec as P

F32, BF16 = jnp.float32, jnp.bfloat16
PITCH, FLIGHT = 12, 4
LANES, HID_LANES, SENT_ROWS = 128, 384, 16
VMEM_LIMIT = 48 * 1024 * 1024
VMEM_SOME = 48_500_000
VMEM_MOST = 62 * 1024 * 1024


def place(routes, here):
    toks = routes.shape[1]
    rows = FLIGHT * PITCH
    slot = lax.broadcasted_iota(jnp.int32, (rows, toks), 0)
    expert = sum((slot >= PITCH * e).astype(jnp.int32) for e in range(1, FLIGHT))
    slot = slot - PITCH * expert
    expert = (expert + here) & (FLIGHT - 1)
    first, second = routes[0:1] == expert, routes[1:2] == expert
    present = jnp.logical_or(first, second)
    earlier = lax.broadcasted_iota(jnp.int32, (toks, toks), 0) < lax.broadcasted_iota(jnp.int32, (toks, toks), 1)
    before = jnp.dot(
        present.astype(F32).astype(BF16), earlier.astype(F32).astype(BF16), preferred_element_type=F32
    )
    taken = jnp.logical_and(present, before == slot.astype(F32))
    return taken, first, second


def rescale(top):
    factor, power = jnp.ones_like(top), jnp.zeros_like(top)
    for bits in (32, 16, 8, 4, 2, 1):
        high = top * (2.0**-bits) >= 8192.0
        scale = jnp.where(high, 2.0**-bits, 1.0)
        top, factor = top * scale, factor * scale
        power = power - jnp.where(high, float(bits), 0.0)
    for bits in (32, 16, 8, 4, 2, 1):
        low = top * (2.0**bits) < 16384.0
        scale = jnp.where(low, 2.0**bits, 1.0)
        top, factor = top * scale, factor * scale
        power = power + jnp.where(low, float(bits), 0.0)
    return factor, power


def dispatch_kernel(here_ref, routes_ref, tokens_ref, out_ref, shrink_ref):
    piece = tokens_ref.shape[1] - out_ref.shape[2]
    chunks = tokens_ref.shape[1] // piece
    taken, _, _ = place(routes_ref[...], here_ref[0])
    taken = taken.astype(F32).astype(BF16)
    picked, top = [], None
    for c in range(chunks):
        columns = tokens_ref[:, c * piece : (c + 1) * piece]
        picked.append(jnp.dot(taken, columns, preferred_element_type=F32))
        most = jnp.max(jnp.abs(picked[c]), axis=1, keepdims=True)
        top = most if top is None else jnp.maximum(top, most)
    grow, _ = rescale(top)
    shrink_ref[...] = 1.0 / grow
    rest = picked[-1] * grow
    for c in range(chunks - 1):
        rows = picked[c] * grow
        for e in range(FLIGHT):
            at = e * PITCH
            tails = [rest[at + i : at + i + 1] for i in range(c, PITCH, chunks - 1)]
            out_ref[e, :, c * piece : (c + 1) * piece] = jnp.concatenate([rows[at : at + PITCH]] + tails, axis=0).astype(BF16)


def dispatch(here, routes_t, tokens):
    width = tokens.shape[1]
    chunks = SENT_ROWS // (SENT_ROWS - PITCH)
    piece = width // chunks
    return pl.pallas_call(
        dispatch_kernel,
        in_specs=[
            pl.BlockSpec(memory_space=pltpu.SMEM),
            pl.BlockSpec(memory_space=pltpu.VMEM),
            pl.BlockSpec(memory_space=pltpu.VMEM),
        ],
        out_shape=(
            jax.ShapeDtypeStruct((FLIGHT, SENT_ROWS, width - piece), BF16),
            jax.ShapeDtypeStruct((FLIGHT * PITCH, 1), F32),
        ),
        compiler_params=pltpu.CompilerParams(vmem_limit_bytes=VMEM_LIMIT),
    )(here, routes_t, tokens)


def unpack_kernel(near_ref, rows_ref):
    short = near_ref.shape[2]
    rest = rows_ref.shape[1] - short
    fold = short // rest
    rows = []
    for e in range(FLIGHT):
        sent = near_ref[e].astype(F32)
        tails = []
        for i in range(PITCH):
            at = PITCH + i // fold
            tails.append(sent[at : at + 1, i % fold * rest : (i % fold + 1) * rest])
        rows.append(jnp.concatenate([sent[:PITCH], jnp.concatenate(tails, axis=0)], axis=1))
    rows_ref[...] = jnp.concatenate(rows, axis=0).astype(BF16)


def unpack(near):
    flight, height, short = near.shape
    return pl.pallas_call(
        unpack_kernel,
        out_shape=jax.ShapeDtypeStruct((flight * PITCH, short * height // PITCH), BF16),
        compiler_params=pltpu.CompilerParams(vmem_limit_bytes=VMEM_LIMIT),
    )(near)


def split_kernel(up_ref, down_ref, out_ref):
    flight, rows, total = up_ref.shape
    wide = out_ref.shape[2]
    blocks = out_ref.shape[0] // flight
    units = total // blocks
    rim = jnp.zeros((rows, wide - units), F32)
    fill = jnp.zeros((rows - total // wide, wide), F32)
    for e in range(flight):
        up, down = up_ref[e].astype(F32), down_ref[e].astype(F32)
        for b in range(blocks):
            top = jnp.concatenate([up[:, b * units : (b + 1) * units], rim], axis=1)
            row = [down[b : b + 1, at : at + wide] for at in range(0, total, wide)]
            out_ref[e * blocks + b] = jnp.concatenate([top] + row + [fill], axis=0).astype(BF16)


def split(up, down, blocks):
    flight, rows, _ = up.shape
    return pl.pallas_call(
        split_kernel,
        out_shape=jax.ShapeDtypeStruct((flight * blocks, 2 * rows, HID_LANES), BF16),
        compiler_params=pltpu.CompilerParams(vmem_limit_bytes=VMEM_MOST),
    )(up, down)


def prepare_kernel(got_ref, noise_ref, out_ref):
    owners, both, wide = got_ref.shape
    rows = both // 2
    units, span = noise_ref.shape
    got = got_ref[...].astype(F32)
    flat = got[:, :rows, :units].reshape(span, units).astype(BF16)
    same = lax.broadcasted_iota(jnp.int32, (span, span), 0) == lax.broadcasted_iota(jnp.int32, (span, span), 1)
    same = same.astype(F32).astype(BF16)
    up = lax.dot_general(flat, same, (((0,), (0,)), ((), ())), preferred_element_type=F32)
    up = (up + noise_ref[...].astype(F32)).astype(BF16)
    for half in range(span // LANES):
        out_ref[half * units : (half + 1) * units] = up[:, half * LANES : (half + 1) * LANES]
    start = span // LANES * units
    per = wide // LANES
    for q in range((out_ref.shape[0] - start) // owners):
        row = got[:, rows + q // per, q % per * LANES : (q % per + 1) * LANES]
        out_ref[start + q * owners : start + (q + 1) * owners] = row.astype(BF16)


def prepare(got, noise_t, total):
    units, span = noise_t.shape
    height = (span * units + got.shape[0] * total) // LANES
    return pl.pallas_call(
        prepare_kernel,
        out_shape=jax.ShapeDtypeStruct((height, LANES), BF16),
        compiler_params=pltpu.CompilerParams(vmem_limit_bytes=VMEM_LIMIT),
    )(got, noise_t)


def up_kernel(x_ref, w_hbm, out_ref, down_ref, w_ref, sems):
    members, height, _ = w_ref.shape
    chunks = sems.shape[0] - 1
    group = members // chunks
    units = height * LANES * members // x_ref.shape[1]
    parts = height // units
    span = parts * LANES
    copies = []
    for c in range(chunks):
        some = slice(c * group, (c + 1) * group)
        copies.append(pltpu.make_async_copy(w_hbm.at[some, :height], w_ref.at[some], sems.at[c]))
    later = pltpu.make_async_copy(w_hbm.at[:, height:], down_ref, sems.at[chunks])
    for copy in copies + [later]:
        copy.start()
    total = None
    for g in range(members):
        if g % group == 0:
            copies[g // group].wait()
        w = jnp.concatenate([w_ref[g, h * units : (h + 1) * units] for h in range(parts)], axis=1)
        x = x_ref[:, g * span : (g + 1) * span]
        term = lax.dot_general(x, w, (((1,), (1,)), ((), ())), preferred_element_type=F32)
        total = term if total is None else total + term
    hidden = jnp.square(jnp.maximum(total, 0.0))
    factor, power = rescale(jnp.max(hidden, axis=1, keepdims=True))
    hidden = hidden.astype(BF16).astype(F32) * factor
    power = jnp.broadcast_to(power, (power.shape[0], out_ref.shape[1] - units))
    out_ref[...] = jnp.concatenate([hidden, power], axis=1).astype(BF16)
    later.wait()


def up_project(x, w, units, chunks=4):
    rows, width = x.shape
    members, both, _ = w.shape
    height = width // members // LANES * units
    return pl.pallas_call(
        up_kernel,
        in_specs=[pl.BlockSpec(memory_space=pltpu.VMEM), pl.BlockSpec(memory_space=pltpu.HBM)],
        out_specs=(pl.BlockSpec(memory_space=pltpu.VMEM), pl.BlockSpec(memory_space=pltpu.VMEM)),
        out_shape=(
            jax.ShapeDtypeStruct((rows, HID_LANES), BF16),
            jax.ShapeDtypeStruct((members, both - height, LANES), BF16),
        ),
        scratch_shapes=[pltpu.VMEM((members, height, LANES), BF16), pltpu.SemaphoreType.DMA((chunks + 1,))],
        compiler_params=pltpu.CompilerParams(vmem_limit_bytes=VMEM_SOME),
        cost_estimate=pl.CostEstimate(flops=2 * rows * width * units, bytes_accessed=2 * width * (rows + units), transcendentals=0),
    )(x, w)


def down_kernel(units, hid_ref, w_ref, out_ref):
    hidden = []
    for b in range(hid_ref.shape[0]):
        h = hid_ref[b].astype(F32)
        hidden.append(h[:, :units] * jnp.exp2(-h[:, units : units + 1]))
    hidden = jnp.concatenate(hidden, axis=1).astype(BF16)
    members, height, _ = w_ref.shape
    tiles = hidden.shape[1] // LANES
    count = height // tiles
    w = [w_ref[:, q * count : (q + 1) * count].reshape(members * count, LANES) for q in range(tiles)]
    w = jnp.concatenate(w, axis=1)
    out = lax.dot_general(hidden, w, (((1,), (1,)), ((), ())), preferred_element_type=F32)
    blocks = out_ref.shape[0] // FLIGHT
    for z in range(blocks):
        for x in range(FLIGHT):
            top = (z * FLIGHT + x) * PITCH
            tiles = [out[top : top + PITCH, t : t + LANES] for t in range(0, out.shape[1], LANES)]
            out_ref[x * blocks + z] = jnp.concatenate(tiles, axis=0).astype(BF16)


def down_project(hid, w, units):
    sources, rows, _ = hid.shape
    total = sources * units
    members, height, _ = w.shape
    cols = members * height * LANES // total
    return pl.pallas_call(
        lambda *r: down_kernel(units, *r),
        out_shape=jax.ShapeDtypeStruct((rows // PITCH, PITCH * cols // LANES, LANES), BF16),
        compiler_params=pltpu.CompilerParams(vmem_limit_bytes=VMEM_LIMIT),
        cost_estimate=pl.CostEstimate(flops=2 * rows * cols * total, bytes_accessed=2 * total * (cols + rows), transcendentals=0),
    )(hid, w)


def mix_kernel(here_ref, routes_ref, gates_ref, shrink_ref, home_ref, out_ref):
    taken, first, second = place(routes_ref[...], here_ref[0])
    gates = gates_ref[...]
    weight = jnp.where(first, gates[0:1], 0.0) + jnp.where(second, gates[1:2], 0.0)
    weight = jnp.where(taken, weight, 0.0) * shrink_ref[...]
    high = weight.astype(BF16)
    rest = weight - high.astype(F32)
    middle = rest.astype(BF16)
    low = rest - middle.astype(F32)
    weight = jnp.concatenate([low, middle.astype(F32), high.astype(F32)], axis=0).astype(BF16)
    owners, height, _ = home_ref.shape
    blocks = owners // FLIGHT
    tiles = height // PITCH
    cols = tiles * LANES
    piece = cols // blocks
    home = []
    for b in range(blocks):
        each = []
        for e in range(FLIGHT):
            tall = home_ref[((here_ref[0] + e) & (FLIGHT - 1)) * blocks + b].astype(F32)
            each.append(jnp.concatenate([tall[t * PITCH : (t + 1) * PITCH] for t in range(tiles)], axis=1))
        home.append(jnp.concatenate(each, axis=0) * shrink_ref[...])
    src = lax.broadcasted_iota(jnp.int32, (cols, cols), 0)
    dst = lax.broadcasted_iota(jnp.int32, (cols, cols), 1)
    order = dst == (src & (piece - 1)) * blocks + (src >> (piece.bit_length() - 1))
    order = order.astype(F32).astype(BF16)
    chunks = [jnp.concatenate([h[:, q * piece : (q + 1) * piece] for h in home], axis=1) for q in range(blocks)]
    count = chunks[0].shape[0]
    chunks = jnp.dot(jnp.concatenate(chunks, axis=0).astype(BF16), order, preferred_element_type=F32).astype(BF16)
    for q in range(blocks):
        chunk = chunks[q * count : (q + 1) * count]
        total = lax.dot_general(
            weight, jnp.concatenate([chunk] * 3, axis=0), (((0,), (0,)), ((), ())), preferred_element_type=F32
        )
        out_ref[:, q * cols : (q + 1) * cols] = total.astype(BF16)


def mix(here, routes_t, gates_t, shrink, home):
    toks = routes_t.shape[1]
    owners, height, _ = home.shape
    width = owners // FLIGHT * height // PITCH * LANES
    return pl.pallas_call(
        mix_kernel,
        in_specs=[pl.BlockSpec(memory_space=pltpu.SMEM)] + [pl.BlockSpec(memory_space=pltpu.VMEM)] * 4,
        out_shape=jax.ShapeDtypeStruct((toks, width), BF16),
        compiler_params=pltpu.CompilerParams(vmem_limit_bytes=VMEM_LIMIT),
    )(here, routes_t, gates_t, shrink, home)


def on_device(tokens, routes, gate_values, dense_up, dense_down, up_noise):
    flight, _, total = dense_up.shape
    units = up_noise.shape[1]
    blocks = total // units
    here = jnp.zeros((1,), jnp.int32)
    mine = lax.axis_index("y") * lax.axis_size("core") + lax.axis_index("core")

    got = lax.all_to_all(split(dense_up, dense_down, blocks), ("x", "z"), 0, 0, tiled=True)

    outgoing, shrink = dispatch(here, routes.T, tokens)
    span = up_noise.shape[0] // lax.axis_size(("y", "core"))
    noise = lax.dynamic_slice_in_dim(up_noise.T, mine * span, span, axis=1)
    got, outgoing, noise = lax.optimization_barrier((got, outgoing, noise))
    shard = prepare(got, noise, total)
    weights = lax.all_gather(shard, ("y", "core"))
    outgoing, _ = lax.optimization_barrier((outgoing, shard))
    near = lax.all_to_all(outgoing, "x", 0, 0, tiled=True)
    routed = unpack(near).astype(jnp.float16)
    routed, _ = lax.optimization_barrier((routed, shard))
    everyone = lax.all_gather(routed, "z", axis=0, tiled=True).astype(BF16)

    hidden, down = up_project(everyone, weights, units)
    hidden = lax.all_gather(hidden.astype(jnp.float16), "z", axis=0, tiled=True).astype(BF16)
    out = down_project(hidden.reshape(blocks, -1, HID_LANES), down, units)
    home = lax.all_to_all(out, ("x", "z"), 0, 0, tiled=True)
    return mix(here, routes.T, gate_values.T, shrink, home)


def solution(mesh):
    split = Mesh(mesh.devices.reshape(8, 2, 4, 8), ("y", "core", "x", "z"))
    every = ("y", "core", "x", "z")
    return jax.shard_map(
        on_device,
        mesh=split,
        in_specs=(
            P(every, None),
            P(every, None),
            P(every, None),
            P(None, every, None),
            P(None, every, None),
            P(None, ("x", "z")),
        ),
        out_specs=P(every, None),
        check_vma=False,
    )
```
